128 devices in a mesh: lat: 16 (over z, x_lo, core), lon: 4 (over y), batch: 2 (over x_hi).
Axes of the slice: x: 4 (x_hi: 2, x_lo: 2; x = x_hi * 2 + x_lo), y: 4, z: 4, core: 2. Of those that a mesh axis runs over, the one named last changes fastest.
Arguments:
- inputs: bfloat16 [4, 128, 360, 1024], P('batch', 'lat', 'lon'), may hold values from -6 to 6
- cotangent: bfloat16 [4, 128, 360, 1024], P('batch', 'lat', 'lon'), may hold values from -6 to 6
- area_weight: float32 [128], P('lat'), may hold values from 0.2 to 2
- first_weight: bfloat16 [2, 8, 128, 128], P(None, 'lon'), may hold values from -0.375 to 0.375
- first_bias: bfloat16 [2, 8, 128], P(None, 'lon'), may hold values from -0.59765625 to 0.59765625
- second_weight: bfloat16 [2, 8, 128, 128], P(None, 'lon'), may hold values from -0.375 to 0.375
- second_bias: bfloat16 [2, 8, 128], P(None, 'lon'), may hold values from -0.59765625 to 0.59765625
Outputs:
- output_field: bfloat16 [4, 128, 360, 1024], P('batch', 'lat', 'lon')
- grad_input: bfloat16 [4, 128, 360, 1024], P('batch', 'lat', 'lon')
- grad_first_weight: float32 [2, 8, 128, 128], P(None, 'lon')
- grad_second_weight: float32 [2, 8, 128, 128], P(None, 'lon')
- grad_first_bias: float32 [2, 8, 128], P(None, 'lon')
- grad_second_bias: float32 [2, 8, 128], P(None, 'lon')
The draws below stay inside these ranges and needn't reach their ends.
All inputs are finite; a program needn't handle non-finite values.
Results may differ from the reference program's by a relative error of at most 0.033.
Values may be sent and summed in bfloat16 or wider, within the bound.
A program may use at most 128 MiB of HBM per device.

```python
import math
import jax
import jax.numpy as jnp
from jax import lax

EMBED = 1024
BLOCKS = 8
LON_CELLS = 360
MODES = 176
BLOCK_WIDTH = 128
LAT_CELLS = 128
MEMBERS = 4


def block_levels(key, shape, pieces, smallest, top_value):
    level, own = 1.0, jax.random.fold_in(key, 6)
    for axis_at, blocks in pieces:
        draws = jnp.exp(jax.random.uniform(jax.random.fold_in(own, axis_at), (blocks,), jnp.float32, smallest / len(pieces), top_value / len(pieces)))
        level = level * jnp.repeat(draws, shape[axis_at] // blocks).reshape([-1 if axis == axis_at else 1 for axis in range(len(shape))])
    return level


def scatter_about(own_key, extent, deviation, bound, pieces=(), kind=jnp.bfloat16):
    loudness = block_levels(own_key, extent, pieces, -0.22, 0.18) if pieces else 1.0
    result = jax.random.normal(own_key, extent, jnp.float32) * deviation * loudness
    return jnp.minimum(jnp.maximum(result, -bound), bound).astype(kind)


def setup_inputs(seed: int = 0) -> dict:
    seeds = jax.random.split(jax.random.key(seed), 8)
    inputs = scatter_about(seeds[0], (MEMBERS, LAT_CELLS, LON_CELLS, EMBED), 1.0, 6.0, ((0, 2), (1, 16), (2, 4)))
    cotangent = scatter_about(seeds[1], (MEMBERS, LAT_CELLS, LON_CELLS, EMBED), 1.0, 6.0, ((0, 2), (1, 16), (2, 4)))
    area_weight = jnp.clip(jnp.exp(math.log(2.0) - 2.3025851 * jax.random.uniform(seeds[2], (LAT_CELLS,), jnp.float32) ** block_levels(seeds[2], (LAT_CELLS,), ((0, 16),), -0.2, 0.2)), 0.2, 2.0)
    first_weight = scatter_about(seeds[3], (2, BLOCKS, BLOCK_WIDTH, BLOCK_WIDTH), (2 * BLOCK_WIDTH) ** -0.5, 0.375, ((1, 4),))
    first_bias = scatter_about(seeds[4], (2, BLOCKS, BLOCK_WIDTH), 0.1, 0.59765625, ((1, 4),))
    second_weight = scatter_about(seeds[5], (2, BLOCKS, BLOCK_WIDTH, BLOCK_WIDTH), (2 * BLOCK_WIDTH) ** -0.5, 0.375, ((1, 4),))
    second_bias = scatter_about(seeds[6], (2, BLOCKS, BLOCK_WIDTH), 0.1, 0.59765625, ((1, 4),))
    return dict(inputs=inputs, cotangent=cotangent, area_weight=area_weight, first_weight=first_weight, first_bias=first_bias, second_weight=second_weight, second_bias=second_bias)


shrink_level = 0.25

def contract(pattern, left, right):
    return jnp.einsum(pattern, left.astype(jnp.float32), right.astype(jnp.float32))

def lon_tables(length, modes_kept):
    column_index = jnp.arange(length, dtype=jnp.int32)[:, None]
    mode_index = jnp.arange(modes_kept, dtype=jnp.int32)[None, :]
    phase_angle = (column_index * mode_index % length).astype(jnp.float32) * (2.0 * math.pi / length)
    scale_factor = 1.0 / math.sqrt(length)
    cosine = jnp.cos(phase_angle) * scale_factor
    sine = jnp.sin(phase_angle) * scale_factor
    forward_table = jnp.stack([cosine, -sine], axis=1)
    mode_weight = jnp.where(mode_index == 0, 1.0, 2.0).astype(jnp.float32)
    inverse_table = jnp.stack([(mode_weight * cosine).T, (-mode_weight * sine).T], axis=0)
    return (forward_table.astype(jnp.bfloat16), inverse_table.astype(jnp.bfloat16))

def lat_table(length):
    row_index = jnp.arange(length, dtype=jnp.int32)
    phase_angle = (row_index[:, None] * row_index[None, :] % length).astype(jnp.float32) * (2.0 * math.pi / length)
    scale_factor = 1.0 / math.sqrt(length)
    cosine = jnp.cos(phase_angle) * scale_factor
    sine = jnp.sin(phase_angle) * scale_factor
    upper = jnp.stack([cosine, -sine], axis=1)
    lower = jnp.stack([sine, cosine], axis=1)
    return jnp.stack([upper, lower], axis=0).astype(jnp.bfloat16)

def spectral_forward(spectrum, first_weight, first_bias, second_weight, second_bias):
    members, lat_modes, parts, lon_modes, channels = spectrum.shape
    block_count = first_weight.shape[1]
    block_width = first_weight.shape[2]
    blocks = spectrum.reshape(members, lat_modes, parts, lon_modes, block_count, block_width)
    real_in = blocks[:, :, 0]
    imag_in = blocks[:, :, 1]
    pattern = 'bmknd,nde->bmkne'
    pre_real = contract(pattern, real_in, first_weight[0]) - contract(pattern, imag_in, first_weight[1]) + first_bias[0].astype(jnp.float32)
    pre_imag = contract(pattern, imag_in, first_weight[0]) + contract(pattern, real_in, first_weight[1]) + first_bias[1].astype(jnp.float32)
    hid_real = jax.nn.gelu(pre_real).astype(jnp.bfloat16)
    hid_imag = jax.nn.gelu(pre_imag).astype(jnp.bfloat16)
    out_real = contract(pattern, hid_real, second_weight[0]) - contract(pattern, hid_imag, second_weight[1]) + second_bias[0].astype(jnp.float32)
    out_imag = contract(pattern, hid_imag, second_weight[0]) + contract(pattern, hid_real, second_weight[1]) + second_bias[1].astype(jnp.float32)
    shrunk_real = out_real - shrink_level * jnp.tanh(out_real / shrink_level)
    shrunk_imag = out_imag - shrink_level * jnp.tanh(out_imag / shrink_level)
    shrunk = jnp.stack([shrunk_real, shrunk_imag], axis=2).reshape(members, lat_modes, parts, lon_modes, channels).astype(jnp.bfloat16)
    saved = (real_in, imag_in, pre_real, pre_imag, hid_real, hid_imag, out_real, out_imag)
    return (shrunk, saved)

def spectral_backward(grad_shrunk, saved, first_weight, second_weight):
    real_in, imag_in, pre_real, pre_imag, hid_real, hid_imag, out_real, out_imag = saved
    members, lat_modes, parts, lon_modes, channels = grad_shrunk.shape
    blocks = grad_shrunk.reshape(members, lat_modes, parts, lon_modes, real_in.shape[3], real_in.shape[4])
    slope_real = jnp.tanh(out_real / shrink_level)
    slope_imag = jnp.tanh(out_imag / shrink_level)
    dout_real = (blocks[:, :, 0].astype(jnp.float32) * slope_real * slope_real).astype(jnp.bfloat16)
    dout_imag = (blocks[:, :, 1].astype(jnp.float32) * slope_imag * slope_imag).astype(jnp.bfloat16)
    over_rows = 'bmknd,bmkne->nde'
    backward = 'bmkne,nde->bmknd'
    gw2_real = contract(over_rows, hid_real, dout_real) + contract(over_rows, hid_imag, dout_imag)
    gw2_imag = contract(over_rows, hid_real, dout_imag) - contract(over_rows, hid_imag, dout_real)
    gb2 = jnp.stack([lax.optimization_barrier(jnp.sum(dout_real.astype(jnp.float32), axis=(0, 1, 2))), lax.optimization_barrier(jnp.sum(dout_imag.astype(jnp.float32), axis=(0, 1, 2)))], axis=0)
    dhid_real = contract(backward, dout_real, second_weight[0]) + contract(backward, dout_imag, second_weight[1])
    dhid_imag = contract(backward, dout_imag, second_weight[0]) - contract(backward, dout_real, second_weight[1])
    dpre_real = jax.vjp(jax.nn.gelu, pre_real)[1](dhid_real)[0].astype(jnp.bfloat16)
    dpre_imag = jax.vjp(jax.nn.gelu, pre_imag)[1](dhid_imag)[0].astype(jnp.bfloat16)
    gw1_real = contract(over_rows, real_in, dpre_real) + contract(over_rows, imag_in, dpre_imag)
    gw1_imag = contract(over_rows, real_in, dpre_imag) - contract(over_rows, imag_in, dpre_real)
    gb1 = jnp.stack([lax.optimization_barrier(jnp.sum(dpre_real.astype(jnp.float32), axis=(0, 1, 2))), lax.optimization_barrier(jnp.sum(dpre_imag.astype(jnp.float32), axis=(0, 1, 2)))], axis=0)
    dspec_real = contract(backward, dpre_real, first_weight[0]) + contract(backward, dpre_imag, first_weight[1])
    dspec_imag = contract(backward, dpre_imag, first_weight[0]) - contract(backward, dpre_real, first_weight[1])
    grad_spectrum = jnp.stack([dspec_real, dspec_imag], axis=2).reshape(members, lat_modes, parts, lon_modes, channels).astype(jnp.bfloat16)
    grad_terms = (jnp.stack([gw1_real, gw1_imag], axis=0), jnp.stack([gw2_real, gw2_imag], axis=0), gb1, gb2)
    return (grad_spectrum, grad_terms)

def reference(inputs, cotangent, area_weight, first_weight, first_bias, second_weight, second_bias):
    members, height, width, channels = inputs.shape
    lon_forward_table, lon_inverse_table = lon_tables(width, MODES)
    lat_square = lat_table(height)

    def one_member(operands):
        member_input = operands[0][None]
        member_cot = operands[1][None]
        weighted = (area_weight[None, :, None, None] * member_cot.astype(jnp.float32)).astype(jnp.bfloat16)
        half_modes = contract('bhwc,wpk->bhpkc', member_input, lon_forward_table).astype(jnp.bfloat16)
        spectrum = contract('bhpkc,phqm->bmqkc', half_modes, lat_square).astype(jnp.bfloat16)
        shrunk, saved = spectral_forward(spectrum, first_weight, first_bias, second_weight, second_bias)
        spatial = contract('bmqkc,phqm->bhpkc', shrunk, lat_square).astype(jnp.bfloat16)
        correction = contract('bhpkc,pkw->bhwc', spatial, lon_inverse_table).astype(jnp.bfloat16)
        field = (member_input.astype(jnp.float32) + correction.astype(jnp.float32)).astype(jnp.bfloat16)
        cot_modes = contract('bhwc,pkw->bhpkc', weighted, lon_inverse_table).astype(jnp.bfloat16)
        cot_spectrum = contract('bhpkc,phqm->bmqkc', cot_modes, lat_square).astype(jnp.bfloat16)
        grad_spectrum, grad_terms = spectral_backward(cot_spectrum, saved, first_weight, second_weight)
        grad_spatial = contract('bmqkc,phqm->bhpkc', grad_spectrum, lat_square).astype(jnp.bfloat16)
        grad_tokens = contract('bhpkc,wpk->bhwc', grad_spatial, lon_forward_table).astype(jnp.bfloat16)
        grad_field = (weighted.astype(jnp.float32) + grad_tokens.astype(jnp.float32)).astype(jnp.bfloat16)
        return (field[0], grad_field[0]) + grad_terms
    results = lax.map(one_member, (inputs, cotangent))
    factor = 1.0 / math.sqrt(members * height * MODES)
    grad_first_weight = lax.optimization_barrier(jnp.sum(results[2], axis=0)) * factor
    grad_second_weight = lax.optimization_barrier(jnp.sum(results[3], axis=0)) * factor
    grad_first_bias = lax.optimization_barrier(jnp.sum(results[4], axis=0)) * factor
    grad_second_bias = lax.optimization_barrier(jnp.sum(results[5], axis=0)) * factor
    return (results[0], results[1], grad_first_weight, grad_second_weight, grad_first_bias, grad_second_bias)
```

```python
import functools
import math

import jax
import jax.numpy as jnp
import numpy as np
from jax import lax
from jax.experimental import pallas as pl
from jax.experimental.pallas import tpu as pltpu
from jax.sharding import PartitionSpec as P

MESH = pl.DeviceIdType.MESH
MODES = 176
LON = 360
LAT = 128
NLAT = 16
NLON = 4
ROWS = 8
MAIN = 80
REST = 10
KL = 11
WINDOW = 32
CHUNKS = 8
HALF = 4
SPAN = 2 * MODES
LINES = KL * LAT
BF = jnp.bfloat16
F32 = jnp.float32


def window_start(h):
    return min(REST * h // 16 * 16, MAIN - WINDOW)


def build_tables():
    w = np.arange(LON)[:, None]
    k = np.arange(MODES)[None, :]
    angle = (w * k % LON).astype(np.float32) * np.float32(2.0 * math.pi / LON)
    cos = np.cos(angle) / math.sqrt(LON)
    sin = np.sin(angle) / math.sqrt(LON)
    weight = np.where(k == 0, 1.0, 2.0)
    forward = np.concatenate([cos, -sin], axis=1)
    back = np.concatenate([weight * cos, -weight * sin], axis=1)

    def arranged(table):
        here = table.reshape(NLON, MAIN + REST, SPAN)
        main = here[:, :MAIN].reshape(NLON * MAIN, SPAN)
        rest = np.zeros((ROWS, NLON, WINDOW, SPAN))
        for h in range(ROWS):
            at = REST * h - window_start(h)
            rest[h, :, at : at + REST] = here[:, MAIN:]
        return main, rest.reshape(ROWS, NLON * WINDOW, SPAN)

    first, second, main_out, rest_out = [], [], [], []
    for there, home in ((forward, back), (back, forward)):
        main, rest = arranged(there)
        first.append(main[:256].T)
        second.append(
            np.stack([np.concatenate([main[256:], rest[h]], axis=0).T for h in range(ROWS)])
        )
        main, rest = arranged(home)
        main_out.append(main)
        rest_out.append(rest)
    h = np.arange(LAT)
    angle = (h[:, None] * h[None, :] % LAT).astype(np.float32) * np.float32(2.0 * math.pi / LAT)
    c = np.cos(angle) / math.sqrt(LAT)
    s = np.sin(angle) / math.sqrt(LAT)
    square = np.stack([np.stack([c, -s], axis=1), np.stack([s, c], axis=1)], axis=0)
    square = square.reshape(2, NLAT, ROWS, 2, LAT).transpose(1, 0, 2, 3, 4).reshape(256, 256)
    cast = lambda a: np.asarray(a, np.float32).astype(jnp.bfloat16)
    return (
        cast(np.stack(first)),
        cast(np.stack(second)),
        cast(np.stack(main_out)),
        cast(np.stack(rest_out)),
        cast(square.T),
        cast(square),
    )


def dot(a, b):
    return jnp.dot(a, b, preferred_element_type=F32)


def dot_tn(a, b):
    return lax.dot_general(a, b, (((0,), (0,)), ((), ())), preferred_element_type=F32)


def kernel(
    x_ref, g_ref, xr_ref, gr_ref, area_ref, w1_ref, b1_ref, w2_ref, b2_ref,
    first_hbm, second_hbm, main_hbm, rest_hbm, latf_ref, latb_ref,
    out_main, out_rest, gw_ref, gb_ref,
    first, second, main_tab, rest_tab,
    ybuf, l1s, l1r, l2s, l2r, y2s, tmp, tmp2, racc,
    sa, hs, gps, sls, shb, dbuf1, dbuf2, wc, wt, bias, acc1, acc2, accb,
    gsend, grecv, xs, xr, ag, brows,
    y1_s, y1_r, l1_s, l1_r, l2_s, l2_r, y2_s, y2_r, t_s, g_s, g_r, p_s, p_r, a_s, a_r,
):
    me = lax.axis_index("lat")
    col = lax.axis_index("lon")
    member = lax.axis_index("batch")

    tables = [
        pltpu.make_async_copy(src, dst, t_s.at[i])
        for i, (src, dst) in enumerate(
            ((first_hbm, first), (second_hbm, second), (main_hbm, main_tab), (rest_hbm, rest_tab))
        )
    ]
    for copy in tables:
        copy.start()

    barrier = pltpu.get_barrier_semaphore()

    def greet_lat(i, _):
        pl.semaphore_signal(
            barrier, inc=1, device_id={"lat": lax.rem(me + i, NLAT)}, device_id_type=MESH
        )
        return 0

    lax.fori_loop(1, NLAT, greet_lat, 0)
    for i in range(1, NLON):
        pl.semaphore_signal(
            barrier, inc=1, device_id={"lon": lax.rem(col + i, NLON)}, device_id_type=MESH
        )
    pl.semaphore_signal(barrier, inc=1, device_id={"batch": 1 - member}, device_id_type=MESH)
    pl.semaphore_wait(barrier, NLAT - 1 + NLON - 1 + 1)

    def place(t):
        c = lax.rem(t, HALF)
        return c // 2, lax.rem(c, 2)

    def y1_from(t, field, rest):
        b, n = place(t)
        for i in (2, 1, 3, 0):
            j = lax.rem(col + i, NLON)
            lanes = pl.ds(pl.multiple_of((2 * j + n) * 128, 128), 128)
            pairs = (
                (field.at[b, :, pl.ds(0, MAIN), lanes], ybuf.at[t, col, pl.ds(0, ROWS)]),
                (rest.at[b, :, lanes], ybuf.at[t, col, ROWS]),
            )
            for src, dst in pairs:
                if i:
                    pltpu.make_async_remote_copy(
                        src, dst, y1_s.at[t], y1_r.at[t],
                        device_id={"lon": j}, device_id_type=MESH,
                    ).start()
                else:
                    pltpu.make_async_copy(src, dst, y1_r.at[t]).start()

    def y1_send(t):
        @pl.when(t < HALF)
        def _():
            y1_from(t, x_ref, xr_ref)

        @pl.when(t >= HALF)
        def _():
            y1_from(t, g_ref, gr_ref)

    def wait_bytes(ref, sem):
        pltpu.make_async_copy(ref, ref, sem).wait()

    y1_send(0)
    y1_send(1)

    for i, ref in enumerate((w1_ref, w2_ref)):
        for n in range(2):
            re = ref[0, n].astype(F32)
            im = ref[1, n].astype(F32)
            whole = jnp.concatenate(
                [jnp.concatenate([re, im], axis=1), jnp.concatenate([-im, re], axis=1)], axis=0
            )
            wc[i, n] = whole.astype(BF)
            wt[i, n] = whole.T.astype(BF)
    for i, ref in enumerate((b1_ref, b2_ref)):
        for n in range(2):
            for q in range(2):
                bias[i, n, :, q * 128 : (q + 1) * 128] = ref[q, n : n + 1].astype(F32)
    acc1[...] = jnp.zeros_like(acc1)
    acc2[...] = jnp.zeros_like(acc2)
    accb[...] = jnp.zeros_like(accb)
    for copy in tables:
        copy.wait()

    def rest_window(h):
        return pl.multiple_of(jnp.minimum(REST * h // 16 * 16, MAIN - WINDOW), 16)

    def stage_a(t):
        kind = t // HALF
        slot = lax.rem(t, 2)
        wait_bytes(ybuf.at[t], y1_r.at[t])

        @pl.when(t + 2 < CHUNKS)
        def _():
            y1_send(t + 2)

        def row(h, _):
            cols = ybuf[t, :, h].reshape(NLON * MAIN, 128)
            rest = ybuf[t, :, ROWS, pl.ds(rest_window(h), WINDOW), :].reshape(NLON * WINDOW, 128)
            tail = jnp.concatenate([cols[256:], rest], axis=0)
            modes = dot(first[kind], cols[:256]) + dot(second[kind, h], tail)
            scale = jnp.where(kind == 0, 1.0, area_ref[h])
            tmp[pl.ds(pl.multiple_of(h * SPAN, 8), SPAN), :] = modes * scale
            return 0

        lax.fori_loop(0, ROWS, row, 0)

        @pl.when(t >= 2)
        def _():
            wait_bytes(l1s.at[slot, pl.ds(0, NLAT - 1)], l1_s.at[t - 2])

        def peer(i, _):
            l = lax.rem(me + i, NLAT)
            for kk in range(KL):
                k = l * KL + kk
                tile = jnp.concatenate(
                    [
                        tmp[pl.ds(k, ROWS, stride=SPAN), :],
                        tmp[pl.ds(k + MODES, ROWS, stride=SPAN), :],
                    ],
                    axis=0,
                ).astype(BF)
                l1s[slot, l, kk] = tile

            @pl.when(i > 0)
            def _():
                pltpu.make_async_remote_copy(
                    l1s.at[slot, l], l1r.at[t, me], l1_s.at[t], l1_r.at[t],
                    device_id={"lat": l}, device_id_type=MESH,
                ).start()

            return 0

        lax.fori_loop(0, NLAT, peer, 0)
        l1r[t, me] = l1s[slot, me]

    def lat_forward(t, out, at):
        def one(k, _):
            z = l1r[t, :, k].reshape(256, 128)
            sp = dot(latf_ref[...], z).astype(BF)
            rows = pl.ds(pl.multiple_of(k * LAT, LAT), LAT)
            view = out.at[at] if at is not None else out
            view[rows, 0:128] = sp[:128]
            view[rows, 128:256] = sp[128:]
            return 0

        lax.fori_loop(0, KL, one, 0)

    def lat_back(t, slot):
        @pl.when(t >= 2)
        def _():
            wait_bytes(l2s.at[slot, pl.ds(0, NLAT - 1)], l2_s.at[t - 2])

        def one(k, _):
            rows = pl.ds(pl.multiple_of(k * LAT, LAT), LAT)
            s = jnp.concatenate([shb[rows, 0:128], shb[rows, 128:256]], axis=0)
            l2s[slot, :, k] = dot(latb_ref[...], s).astype(BF).reshape(NLAT, 16, 128)
            return 0

        lax.fori_loop(0, KL, one, 0)

        def peer(i, _):
            l = lax.rem(me + i, NLAT)
            pltpu.make_async_remote_copy(
                l2s.at[slot, l], l2r.at[t, me], l2_s.at[t], l2_r.at[t],
                device_id={"lat": l}, device_id_type=MESH,
            ).start()
            return 0

        lax.fori_loop(1, NLAT, peer, 0)
        l2r[t, me] = l2s[slot, me]

    BLOCK = 176
    C0 = math.sqrt(2.0 / math.pi)
    C1 = C0 * 0.044715

    def stage_b_forward(t):
        n = lax.rem(t, 2)
        slot = lax.rem(t, 2)
        lat_forward(t, sa, t)

        def one(i, _):
            rows = pl.ds(pl.multiple_of(i * BLOCK, 16), BLOCK)
            u = dot(sa[t, rows], wc[0, n]) + bias[0, n]
            sq = u * u
            th = jnp.tanh(u * (C0 + C1 * sq))
            half = 0.5 + 0.5 * th
            hid = (u * half).astype(BF)
            hs[t, rows] = hid
            gps[t, rows] = half + (0.5 * u) * (1.0 - th * th) * (C0 + (3.0 * C1) * sq)
            o = dot(hid, wc[1, n]) + bias[1, n]
            slope = jnp.tanh(o * 4.0)
            sls[t, rows] = slope * slope
            shb[rows] = (o - 0.25 * slope).astype(BF)
            return 0

        lax.fori_loop(0, LINES // BLOCK, one, 0)
        lat_back(t, slot)

    def stage_b_backward(t):
        c = t - HALF
        n = lax.rem(t, 2)
        slot = lax.rem(t, 2)
        lat_forward(t, dbuf2, None)

        def one(i, _):
            rows = pl.ds(pl.multiple_of(i * BLOCK, 16), BLOCK)
            d = (dbuf2[rows].astype(F32) * sls[c, rows]).astype(BF)
            dbuf2[rows] = d
            dp = (dot(d, wt[1, n]) * gps[c, rows]).astype(BF)
            dbuf1[rows] = dp
            shb[rows] = dot(dp, wt[0, n]).astype(BF)
            accb[n, 0] += jnp.sum(dp.astype(F32), axis=0, keepdims=True)
            accb[n, 1] += jnp.sum(d.astype(F32), axis=0, keepdims=True)
            return 0

        lax.fori_loop(0, LINES // BLOCK, one, 0)
        lat_back(t, slot)
        acc1[n] += dot_tn(sa[c], dbuf1[...])
        acc2[n] += dot_tn(hs[c], dbuf2[...])

    def stage_c(t):
        kind = t // HALF
        slot = lax.rem(t, 2)
        b, n = place(t)
        wait_bytes(l2r.at[t, pl.ds(0, NLAT - 1)], l2_r.at[t])

        def peer(l, _):
            for kk in range(KL):
                k = l * KL + kk
                v = l2r[t, l, kk].astype(F32)
                tmp2[pl.ds(k, ROWS, stride=SPAN), :] = v[:ROWS]
                tmp2[pl.ds(k + MODES, ROWS, stride=SPAN), :] = v[ROWS:]
            return 0

        lax.fori_loop(0, NLAT, peer, 0)

        @pl.when(t >= 2)
        def _():
            wait_bytes(y2s.at[slot], y2_s.at[t - 2])

        racc[...] = jnp.zeros_like(racc)

        def row(h, _):
            s = tmp2[pl.ds(pl.multiple_of(h * SPAN, 8), SPAN), :].astype(BF)
            y2s[slot, :, h] = dot(main_tab[kind], s).astype(BF).reshape(NLON, MAIN, 128)
            racc[:, pl.ds(rest_window(h), WINDOW), :] += dot(rest_tab[kind, h], s).reshape(
                NLON, WINDOW, 128
            )
            return 0

        lax.fori_loop(0, ROWS, row, 0)
        y2s[slot, :, ROWS] = racc[...].astype(BF)
        lanes = pl.ds(pl.multiple_of((2 * col + n) * 128, 128), 128)
        for i in (2, 1, 3, 0):
            j = lax.rem(col + i, NLON)
            pairs = (
                (y2s.at[slot, j, pl.ds(0, ROWS)], out_main.at[kind, b, :, :, lanes]),
                (y2s.at[slot, j, ROWS], out_rest.at[kind, b, :, lanes]),
            )
            for src, dst in pairs:
                if i:
                    pltpu.make_async_remote_copy(
                        src, dst, y2_s.at[t], y2_r.at[t],
                        device_id={"lon": j}, device_id_type=MESH,
                    ).start()
                else:
                    pltpu.make_async_copy(src, dst, y2_s.at[t]).start()

    def scatter_grads():
        gsend[...] = jnp.zeros_like(gsend)
        brows[...] = jnp.zeros_like(brows)
        for which, acc in enumerate((acc1, acc2)):
            for n in range(2):
                a = acc[n]
                parts = (
                    a[:128, :128] + a[128:, 128:],
                    a[:128, 128:] - a[128:, :128],
                )
                for q in range(2):
                    at = (which * 2 + q) * 2 + n
                    part = parts[q].astype(BF)
                    gsend[2 * at, 0:64] = part[:64]
                    gsend[2 * at + 1, 0:64] = part[64:]
                    brows[at : at + 1, :] = accb[n, which, :, q * 128 : (q + 1) * 128]
        gsend[0, 64:80] = brows[...].astype(BF)

        def peer(i, _):
            l = lax.rem(me + i, NLAT)
            pltpu.make_async_remote_copy(
                gsend.at[l], grecv.at[me], g_s, g_r,
                device_id={"lat": l}, device_id_type=MESH,
            ).start()
            return 0

        lax.fori_loop(1, NLAT, peer, 0)
        grecv[me] = gsend[me]

    def finish_grads():
        wait_bytes(grecv.at[pl.ds(0, NLAT - 1)], g_r)
        part = grecv[0].astype(F32)
        for l in range(1, NLAT):
            part = part + grecv[l].astype(F32)
        xs[...] = part
        swap = pltpu.make_async_remote_copy(
            xs, xr, p_s, p_r, device_id={"batch": 1 - member}, device_id_type=MESH
        )
        swap.start()
        swap.wait()
        factor = 1.0 / math.sqrt(4 * LAT * MODES)
        ag[me] = ((xs[...] + xr[...]) * factor).astype(BF)

        def peer(i, _):
            l = lax.rem(me + i, NLAT)
            pltpu.make_async_remote_copy(
                ag.at[me], ag.at[me], a_s, a_r,
                device_id={"lat": l}, device_id_type=MESH,
            ).start()
            return 0

        lax.fori_loop(1, NLAT, peer, 0)
        wait_bytes(ag.at[pl.ds(0, NLAT - 1)], a_r)
        for l in range(NLAT):
            gw_ref[l * 64 : (l + 1) * 64, :] = ag[l, 0:64].astype(F32)
        gb_ref[...] = ag[0, 64:80].astype(F32)[:8]
        wait_bytes(ag.at[pl.ds(0, NLAT - 1)], a_s)
        wait_bytes(gsend.at[pl.ds(0, NLAT - 1)], g_s)

    def slot_of(s, _):
        @pl.when(s < CHUNKS)
        def _():
            stage_a(s)

        @pl.when(jnp.logical_and(s >= 1, s <= CHUNKS))
        def _():
            t = s - 1
            wait_bytes(l1r.at[t, pl.ds(0, NLAT - 1)], l1_r.at[t])

            @pl.when(t < HALF)
            def _():
                stage_b_forward(t)

            @pl.when(t >= HALF)
            def _():
                stage_b_backward(t)

        @pl.when(s == CHUNKS)
        def _():
            scatter_grads()

        @pl.when(s >= 2)
        def _():
            stage_c(s - 2)

        return 0

    lax.fori_loop(0, CHUNKS + 2, slot_of, 0)
    finish_grads()
    for t in range(CHUNKS):
        wait_bytes(ybuf.at[t, pl.ds(0, NLON - 1)], y1_s.at[t])
        wait_bytes(ybuf.at[t, pl.ds(0, NLON - 1)], y2_r.at[t])
    for t in (CHUNKS - 2, CHUNKS - 1):
        wait_bytes(l1s.at[t % 2, pl.ds(0, NLAT - 1)], l1_s.at[t])
        wait_bytes(l2s.at[t % 2, pl.ds(0, NLAT - 1)], l2_s.at[t])
        wait_bytes(y2s.at[t % 2], y2_s.at[t])


def per_device(inputs, cotangent, area, w1, b1, w2, b2):
    members, rows, cols, channels = inputs.shape
    tables = [jnp.asarray(a) for a in build_tables()]
    x_rest = inputs[:, :, MAIN:, :].reshape(members, rows * REST, channels)
    g_rest = cotangent[:, :, MAIN:, :].reshape(members, rows * REST, channels)
    anywhere = pl.BlockSpec(memory_space=pl.ANY)
    vmem = pl.BlockSpec(memory_space=pltpu.VMEM)
    smem = pl.BlockSpec(memory_space=pltpu.SMEM)
    dma = pltpu.SemaphoreType.DMA
    V = pltpu.VMEM
    out_main, out_rest, gw, gb = pl.pallas_call(
        kernel,
        out_shape=(
            jax.ShapeDtypeStruct((2, members, rows, MAIN, channels), BF),
            jax.ShapeDtypeStruct((2, members, rows * REST, channels), BF),
            jax.ShapeDtypeStruct((1024, 128), F32),
            jax.ShapeDtypeStruct((8, 128), F32),
        ),
        in_specs=[anywhere] * 4 + [smem] + [vmem] * 4 + [anywhere] * 4 + [vmem] * 2,
        out_specs=(anywhere, anywhere, vmem, vmem),
        scratch_shapes=[
            V((2, SPAN, 256), BF),
            V((2, ROWS, SPAN, 192), BF),
            V((2, NLON * MAIN, SPAN), BF),
            V((2, ROWS, NLON * WINDOW, SPAN), BF),
            V((CHUNKS, NLON, ROWS + 1, MAIN, 128), BF),
            V((2, NLAT, KL, 16, 128), BF),
            V((CHUNKS, NLAT, KL, 16, 128), BF),
            V((2, NLAT, KL, 16, 128), BF),
            V((CHUNKS, NLAT, KL, 16, 128), BF),
            V((2, NLON, ROWS + 1, MAIN, 128), BF),
            V((ROWS * SPAN, 128), F32),
            V((ROWS * SPAN, 128), F32),
            V((NLON, MAIN, 128), F32),
            V((HALF, LINES, 256), BF),
            V((HALF, LINES, 256), BF),
            V((HALF, LINES, 256), F32),
            V((HALF, LINES, 256), F32),
            V((LINES, 256), BF),
            V((LINES, 256), BF),
            V((LINES, 256), BF),
            V((2, 2, 256, 256), BF),
            V((2, 2, 256, 256), BF),
            V((2, 2, 1, 256), F32),
            V((2, 256, 256), F32),
            V((2, 256, 256), F32),
            V((2, 2, 1, 256), F32),
            V((NLAT, 80, 128), BF),
            V((NLAT, 80, 128), BF),
            V((80, 128), F32),
            V((80, 128), F32),
            V((NLAT, 80, 128), BF),
            V((16, 128), F32),
        ]
        + [dma((CHUNKS,))] * 8
        + [dma((4,))]
        + [dma(())] * 6,
        compiler_params=pltpu.CompilerParams(
            collective_id=0, has_side_effects=True, vmem_limit_bytes=60 * 2**20
        ),
        name="afno",
    )(inputs, cotangent, x_rest, g_rest, area, w1, b1, w2, b2, *tables)

    def whole(kind):
        rest = out_rest[kind].reshape(members, rows, REST, channels)
        return jnp.concatenate([out_main[kind], rest], axis=2).astype(F32)

    weighted = (area[None, :, None, None] * cotangent.astype(F32)).astype(BF)
    output_field = (inputs.astype(F32) + whole(0)).astype(BF)
    grad_input = (weighted.astype(F32) + whole(1)).astype(BF)
    gw = gw.reshape(2, 2, 2, 128, 128)
    gb = gb.reshape(2, 2, 2, 128)
    return output_field, grad_input, gw[0], gw[1], gb[0], gb[1]


def solution(mesh):
    return jax.shard_map(
        per_device,
        mesh=mesh,
        in_specs=(
            P("batch", "lat", "lon", None),
            P("batch", "lat", "lon", None),
            P("lat"),
            P(None, "lon", None, None),
            P(None, "lon", None),
            P(None, "lon", None, None),
            P(None, "lon", None),
        ),
        out_specs=(
            P("batch", "lat", "lon", None),
            P("batch", "lat", "lon", None),
            P(None, "lon", None, None),
            P(None, "lon", None, None),
            P(None, "lon", None),
            P(None, "lon", None),
        ),
        check_vma=False,
    )
```

```python
import functools
import math

import jax
import jax.numpy as jnp
import numpy as np
from jax import lax
from jax.experimental import pallas as pl
from jax.experimental.pallas import tpu as pltpu
from jax.sharding import PartitionSpec as P

MESH = pl.DeviceIdType.MESH
MODES = 176
LON = 360
LAT = 128
NLAT = 16
NLON = 4
ROWS = 8
COLS = LON // NLON
AREA = COLS * ROWS
KL = 11
CHUNKS = 8
HALF = 4
SPAN = 2 * MODES
LINES = KL * LAT
BF = jnp.bfloat16
F32 = jnp.float32


def build_tables():
    w = np.arange(LON)[:, None]
    k = np.arange(MODES)[None, :]
    angle = (w * k % LON).astype(np.float32) * np.float32(2.0 * math.pi / LON)
    cos = np.cos(angle) / math.sqrt(LON)
    sin = np.sin(angle) / math.sqrt(LON)
    weight = np.where(k == 0, 1.0, 2.0)
    forward = np.concatenate([cos, -sin], axis=1)
    back = np.concatenate([weight * cos, -weight * sin], axis=1)
    h = np.arange(LAT)
    angle = (h[:, None] * h[None, :] % LAT).astype(np.float32) * np.float32(2.0 * math.pi / LAT)
    c = np.cos(angle) / math.sqrt(LAT)
    s = np.sin(angle) / math.sqrt(LAT)
    square = np.stack([np.stack([c, -s], axis=1), np.stack([s, c], axis=1)], axis=0)
    square = square.reshape(2, NLAT, ROWS, 2, LAT).transpose(1, 0, 2, 3, 4).reshape(256, 256)
    cast = lambda a: np.asarray(a, np.float32).astype(jnp.bfloat16)
    return (
        cast(np.stack([forward.T, back.T])),
        cast(np.stack([back, forward])),
        cast(square.T),
        cast(square),
    )


def dot(a, b):
    return jnp.dot(a, b, preferred_element_type=F32)


def dot_tn(a, b):
    return lax.dot_general(a, b, (((0,), (0,)), ((), ())), preferred_element_type=F32)


def kernel(
    x_ref, g_ref, area_ref, w1_ref, b1_ref, w2_ref, b2_ref,
    lonf_hbm, lonb_hbm, latf_ref, latb_ref,
    outx_ref, outg_ref, gw1_ref, gw2_ref, gb1_ref, gb2_ref,
    lonf, lonb,
    ybuf, l1s, l1r, l2s, l2r, y2s, tmp, tmp2, cells, cells2,
    sa, hs, gps, sls, shb, dbuf1, dbuf2, wc, wt, bias, acc1, acc2, accb,
    gsend, grecv, xs, xr, ag, brows,
    y1_s, y1_r, l1_s, l1_r, l2_s, l2_r, y2_s, y2_r, t_s, g_s, g_r, p_s, p_r, a_s, a_r,
):
    me = lax.axis_index("lat")
    col = lax.axis_index("lon")
    member = lax.axis_index("batch")

    tables = [
        pltpu.make_async_copy(src, dst, t_s.at[i])
        for i, (src, dst) in enumerate(
            ((lonf_hbm, lonf), (lonb_hbm, lonb))
        )
    ]
    for copy in tables:
        copy.start()

    barrier = pltpu.get_barrier_semaphore()

    def greet_lat(i, _):
        pl.semaphore_signal(
            barrier, inc=1, device_id={"lat": lax.rem(me + i, NLAT)}, device_id_type=MESH
        )
        return 0

    lax.fori_loop(1, NLAT, greet_lat, 0)
    for i in range(1, NLON):
        pl.semaphore_signal(
            barrier, inc=1, device_id={"lon": lax.rem(col + i, NLON)}, device_id_type=MESH
        )
    pl.semaphore_signal(barrier, inc=1, device_id={"batch": 1 - member}, device_id_type=MESH)
    pl.semaphore_wait(barrier, NLAT - 1 + NLON - 1 + 1)

    def place(t):
        c = lax.rem(t, HALF)
        return c // 2, lax.rem(c, 2)

    def y1_from(t, field):
        b, n = place(t)
        for i in (2, 1, 3, 0):
            j = lax.rem(col + i, NLON)
            lanes = pl.ds(pl.multiple_of((2 * j + n) * 128, 128), 128)
            src, dst = field.at[b, :, lanes], ybuf.at[t, col]
            if i:
                pltpu.make_async_remote_copy(
                    src, dst, y1_s.at[t], y1_r.at[t],
                    device_id={"lon": j}, device_id_type=MESH,
                ).start()
            else:
                pltpu.make_async_copy(src, dst, y1_r.at[t]).start()

    def y1_send(t):
        @pl.when(t < HALF)
        def _():
            y1_from(t, x_ref)

        @pl.when(t >= HALF)
        def _():
            y1_from(t, g_ref)

    def wait_bytes(ref, sem):
        pltpu.make_async_copy(ref, ref, sem).wait()

    y1_send(0)
    y1_send(1)

    for i, ref in enumerate((w1_ref, w2_ref)):
        for n in range(2):
            re = ref[0, n].astype(F32)
            im = ref[1, n].astype(F32)
            whole = jnp.concatenate(
                [jnp.concatenate([re, im], axis=1), jnp.concatenate([-im, re], axis=1)], axis=0
            )
            wc[i, n] = whole.astype(BF)
            wt[i, n] = whole.T.astype(BF)
    for i, ref in enumerate((b1_ref, b2_ref)):
        for n in range(2):
            for q in range(2):
                bias[i, n, :, q * 128 : (q + 1) * 128] = ref[q, n : n + 1].astype(F32)
    acc1[...] = jnp.zeros_like(acc1)
    acc2[...] = jnp.zeros_like(acc2)
    accb[...] = jnp.zeros_like(accb)
    for copy in tables:
        copy.wait()

    def stage_a(t):
        kind = t // HALF
        slot = lax.rem(t, 2)
        wait_bytes(ybuf.at[t], y1_r.at[t])

        @pl.when(t + 2 < CHUNKS)
        def _():
            y1_send(t + 2)

        for j in range(NLON):
            cells[j * AREA : (j + 1) * AREA, :] = ybuf[t, j].astype(F32)

        def rows(i, _):
            h = 2 * i
            field = jnp.concatenate(
                [cells[pl.ds(h + q, LON, stride=ROWS), :].astype(BF) for q in range(2)], axis=1
            )
            modes = dot(lonf[kind], field)
            for q in range(2):
                scale = jnp.where(kind == 0, 1.0, area_ref[h + q])
                tmp[pl.ds(h + q, SPAN, stride=ROWS), :] = modes[:, q * 128 : (q + 1) * 128] * scale
            return 0

        lax.fori_loop(0, ROWS // 2, rows, 0)

        @pl.when(t >= 2)
        def _():
            wait_bytes(l1s.at[slot, pl.ds(0, NLAT - 1)], l1_s.at[t - 2])

        def peer(i, _):
            l = lax.rem(me + i, NLAT)
            at = pl.multiple_of(l * (KL * ROWS), ROWS)
            both = [
                tmp[pl.ds(at + p * (MODES * ROWS), KL * ROWS), :].reshape(KL, ROWS, 128)
                for p in range(2)
            ]
            l1s[slot, l] = jnp.concatenate(both, axis=1).astype(BF)

            @pl.when(i > 0)
            def _():
                pltpu.make_async_remote_copy(
                    l1s.at[slot, l], l1r.at[t, me], l1_s.at[t], l1_r.at[t],
                    device_id={"lat": l}, device_id_type=MESH,
                ).start()

            return 0

        lax.fori_loop(0, NLAT, peer, 0)
        l1r[t, me] = l1s[slot, me]

    def lat_forward(t, out, at):
        def one(k, _):
            z = l1r[t, :, k].reshape(256, 128)
            sp = dot(latf_ref[...], z).astype(BF)
            rows = pl.ds(pl.multiple_of(k * LAT, LAT), LAT)
            view = out.at[at] if at is not None else out
            view[rows, 0:128] = sp[:128]
            view[rows, 128:256] = sp[128:]
            return 0

        lax.fori_loop(0, KL, one, 0)

    def lat_back(t, slot):
        @pl.when(t >= 2)
        def _():
            wait_bytes(l2s.at[slot, pl.ds(0, NLAT - 1)], l2_s.at[t - 2])

        def one(k, _):
            rows = pl.ds(pl.multiple_of(k * LAT, LAT), LAT)
            s = jnp.concatenate([shb[rows, 0:128], shb[rows, 128:256]], axis=0)
            l2s[slot, :, k] = dot(latb_ref[...], s).astype(BF).reshape(NLAT, 16, 128)
            return 0

        lax.fori_loop(0, KL, one, 0)

        def peer(i, _):
            l = lax.rem(me + i, NLAT)
            pltpu.make_async_remote_copy(
                l2s.at[slot, l], l2r.at[t, me], l2_s.at[t], l2_r.at[t],
                device_id={"lat": l}, device_id_type=MESH,
            ).start()
            return 0

        lax.fori_loop(1, NLAT, peer, 0)
        l2r[t, me] = l2s[slot, me]

    BLOCK = 176
    C0 = math.sqrt(2.0 / math.pi)
    C1 = C0 * 0.044715

    def stage_b_forward(t):
        n = lax.rem(t, 2)
        slot = lax.rem(t, 2)
        lat_forward(t, sa, t)

        def one(i, _):
            rows = pl.ds(pl.multiple_of(i * BLOCK, 16), BLOCK)
            u = dot(sa[t, rows], wc[0, n]) + bias[0, n]
            sq = u * u
            th = jnp.tanh(u * (C0 + C1 * sq))
            half = 0.5 + 0.5 * th
            hid = (u * half).astype(BF)
            hs[t, rows] = hid
            gps[t, rows] = half + (0.5 * u) * (1.0 - th * th) * (C0 + (3.0 * C1) * sq)
            o = dot(hid, wc[1, n]) + bias[1, n]
            slope = jnp.tanh(o * 4.0)
            sls[t, rows] = slope * slope
            shb[rows] = (o - 0.25 * slope).astype(BF)
            return 0

        lax.fori_loop(0, LINES // BLOCK, one, 0)
        lat_back(t, slot)

    def stage_b_backward(t):
        c = t - HALF
        n = lax.rem(t, 2)
        slot = lax.rem(t, 2)
        lat_forward(t, dbuf2, None)

        def one(i, _):
            rows = pl.ds(pl.multiple_of(i * BLOCK, 16), BLOCK)
            d = (dbuf2[rows].astype(F32) * sls[c, rows]).astype(BF)
            dbuf2[rows] = d
            dp = (dot(d, wt[1, n]) * gps[c, rows]).astype(BF)
            dbuf1[rows] = dp
            shb[rows] = dot(dp, wt[0, n]).astype(BF)
            accb[n, 0] += jnp.sum(dp.astype(F32), axis=0, keepdims=True)
            accb[n, 1] += jnp.sum(d.astype(F32), axis=0, keepdims=True)
            return 0

        lax.fori_loop(0, LINES // BLOCK, one, 0)
        lat_back(t, slot)
        acc1[n] += dot_tn(sa[c], dbuf1[...])
        acc2[n] += dot_tn(hs[c], dbuf2[...])

    def stage_c(t):
        kind = t // HALF
        slot = lax.rem(t, 2)
        b, n = place(t)
        wait_bytes(l2r.at[t, pl.ds(0, NLAT - 1)], l2_r.at[t])

        def peer(l, _):
            v = l2r[t, l].astype(F32)
            at = pl.multiple_of(l * (KL * ROWS), ROWS)
            for p in range(2):
                half = v[:, p * ROWS : (p + 1) * ROWS].reshape(KL * ROWS, 128)
                tmp2[pl.ds(at + p * (MODES * ROWS), KL * ROWS), :] = half
            return 0

        lax.fori_loop(0, NLAT, peer, 0)

        @pl.when(t >= 2)
        def _():
            wait_bytes(y2s.at[slot], y2_s.at[t - 2])

        def rows(i, _):
            h = 2 * i
            modes = jnp.concatenate(
                [tmp2[pl.ds(h + q, SPAN, stride=ROWS), :].astype(BF) for q in range(2)], axis=1
            )
            field = dot(lonb[kind], modes)
            for q in range(2):
                cells2[pl.ds(h + q, LON, stride=ROWS), :] = field[:, q * 128 : (q + 1) * 128]
            return 0

        lax.fori_loop(0, ROWS // 2, rows, 0)
        for j in range(NLON):
            y2s[slot, j] = cells2[j * AREA : (j + 1) * AREA, :].astype(BF)
        lanes = pl.ds(pl.multiple_of((2 * col + n) * 128, 128), 128)

        def y2_to(out):
            for i in (2, 1, 3, 0):
                j = lax.rem(col + i, NLON)
                src, dst = y2s.at[slot, j], out.at[b, :, lanes]
                if i:
                    pltpu.make_async_remote_copy(
                        src, dst, y2_s.at[t], y2_r.at[t],
                        device_id={"lon": j}, device_id_type=MESH,
                    ).start()
                else:
                    pltpu.make_async_copy(src, dst, y2_s.at[t]).start()

        @pl.when(kind == 0)
        def _():
            y2_to(outx_ref)

        @pl.when(kind == 1)
        def _():
            y2_to(outg_ref)

    def scatter_grads():
        gsend[...] = jnp.zeros_like(gsend)
        brows[...] = jnp.zeros_like(brows)
        for which, acc in enumerate((acc1, acc2)):
            for n in range(2):
                a = acc[n]
                parts = (
                    a[:128, :128] + a[128:, 128:],
                    a[:128, 128:] - a[128:, :128],
                )
                for q in range(2):
                    at = (which * 2 + q) * 2 + n
                    part = parts[q].astype(BF)
                    gsend[2 * at, 0:64] = part[:64]
                    gsend[2 * at + 1, 0:64] = part[64:]
                    brows[at : at + 1, :] = accb[n, which, :, q * 128 : (q + 1) * 128]
        gsend[0, 64:80] = brows[...].astype(BF)

        def peer(i, _):
            l = lax.rem(me + i, NLAT)
            pltpu.make_async_remote_copy(
                gsend.at[l], grecv.at[me], g_s, g_r,
                device_id={"lat": l}, device_id_type=MESH,
            ).start()
            return 0

        lax.fori_loop(1, NLAT, peer, 0)
        grecv[me] = gsend[me]

    def finish_grads():
        wait_bytes(grecv.at[pl.ds(0, NLAT - 1)], g_r)
        part = grecv[0].astype(F32)
        for l in range(1, NLAT):
            part = part + grecv[l].astype(F32)
        xs[...] = part
        swap = pltpu.make_async_remote_copy(
            xs, xr, p_s, p_r, device_id={"batch": 1 - member}, device_id_type=MESH
        )
        swap.start()
        swap.wait()
        factor = 1.0 / math.sqrt(4 * LAT * MODES)
        ag[me] = ((xs[...] + xr[...]) * factor).astype(BF)

        def peer(i, _):
            l = lax.rem(me + i, NLAT)
            pltpu.make_async_remote_copy(
                ag.at[me], ag.at[me], a_s, a_r,
                device_id={"lat": l}, device_id_type=MESH,
            ).start()
            return 0

        lax.fori_loop(1, NLAT, peer, 0)
        wait_bytes(ag.at[pl.ds(0, NLAT - 1)], a_r)
        for l in range(NLAT):
            out = (gw1_ref, gw2_ref)[l // 8]
            out[l % 8 // 4, l % 4 // 2, l % 2 * 64 : (l % 2 + 1) * 64, :] = ag[l, 0:64].astype(F32)
        biases = ag[0, 64:80].astype(F32)
        for at in range(8):
            out = (gb1_ref, gb2_ref)[at // 4]
            out[at % 4 // 2, at % 2 : at % 2 + 1, :] = biases[at : at + 1]
        wait_bytes(ag.at[pl.ds(0, NLAT - 1)], a_s)
        wait_bytes(gsend.at[pl.ds(0, NLAT - 1)], g_s)

    def slot_of(s, _):
        @pl.when(s < CHUNKS)
        def _():
            stage_a(s)

        @pl.when(jnp.logical_and(s >= 1, s <= CHUNKS))
        def _():
            t = s - 1
            wait_bytes(l1r.at[t, pl.ds(0, NLAT - 1)], l1_r.at[t])

            @pl.when(t < HALF)
            def _():
                stage_b_forward(t)

            @pl.when(t >= HALF)
            def _():
                stage_b_backward(t)

        @pl.when(s == CHUNKS)
        def _():
            scatter_grads()

        @pl.when(s >= 2)
        def _():
            stage_c(s - 2)

        return 0

    lax.fori_loop(0, CHUNKS + 2, slot_of, 0)
    finish_grads()
    for t in range(CHUNKS):
        wait_bytes(ybuf.at[t, pl.ds(0, NLON - 1)], y1_s.at[t])
        wait_bytes(ybuf.at[t, pl.ds(0, NLON - 1)], y2_r.at[t])
    for t in (CHUNKS - 2, CHUNKS - 1):
        wait_bytes(l1s.at[t % 2, pl.ds(0, NLAT - 1)], l1_s.at[t])
        wait_bytes(l2s.at[t % 2, pl.ds(0, NLAT - 1)], l2_s.at[t])
        wait_bytes(y2s.at[t % 2], y2_s.at[t])


def per_device(inputs, cotangent, area, w1, b1, w2, b2):
    members, rows, cols, channels = inputs.shape
    tables = [jnp.asarray(a) for a in build_tables()]

    def merged(field):
        return field.transpose(0, 2, 1, 3).reshape(members, cols * rows, channels)

    x, g = merged(inputs), merged(cotangent)
    anywhere = pl.BlockSpec(memory_space=pl.ANY)
    vmem = pl.BlockSpec(memory_space=pltpu.VMEM)
    smem = pl.BlockSpec(memory_space=pltpu.SMEM)
    dma = pltpu.SemaphoreType.DMA
    V = pltpu.VMEM
    correction, back, gw1, gw2, gb1, gb2 = pl.pallas_call(
        kernel,
        out_shape=(
            jax.ShapeDtypeStruct(x.shape, BF),
            jax.ShapeDtypeStruct(g.shape, BF),
            jax.ShapeDtypeStruct(w1.shape, F32),
            jax.ShapeDtypeStruct(w2.shape, F32),
            jax.ShapeDtypeStruct(b1.shape, F32),
            jax.ShapeDtypeStruct(b2.shape, F32),
        ),
        in_specs=[anywhere] * 2 + [smem] + [vmem] * 4 + [anywhere] * 2 + [vmem] * 2,
        out_specs=(anywhere, anywhere, vmem, vmem, vmem, vmem),
        scratch_shapes=[
            V((2, SPAN, LON), BF),
            V((2, LON, SPAN), BF),
            V((CHUNKS, NLON, AREA, 128), BF),
            V((2, NLAT, KL, 16, 128), BF),
            V((CHUNKS, NLAT, KL, 16, 128), BF),
            V((2, NLAT, KL, 16, 128), BF),
            V((CHUNKS, NLAT, KL, 16, 128), BF),
            V((2, NLON, AREA, 128), BF),
            V((ROWS * SPAN, 128), F32),
            V((ROWS * SPAN, 128), F32),
            V((LON * ROWS, 128), F32),
            V((LON * ROWS, 128), F32),
            V((HALF, LINES, 256), BF),
            V((HALF, LINES, 256), BF),
            V((HALF, LINES, 256), F32),
            V((HALF, LINES, 256), F32),
            V((LINES, 256), BF),
            V((LINES, 256), BF),
            V((LINES, 256), BF),
            V((2, 2, 256, 256), BF),
            V((2, 2, 256, 256), BF),
            V((2, 2, 1, 256), F32),
            V((2, 256, 256), F32),
            V((2, 256, 256), F32),
            V((2, 2, 1, 256), F32),
            V((NLAT, 80, 128), BF),
            V((NLAT, 80, 128), BF),
            V((80, 128), F32),
            V((80, 128), F32),
            V((NLAT, 80, 128), BF),
            V((16, 128), F32),
        ]
        + [dma((CHUNKS,))] * 8
        + [dma((2,))]
        + [dma(())] * 6,
        compiler_params=pltpu.CompilerParams(
            collective_id=0, has_side_effects=True, vmem_limit_bytes=60 * 2**20
        ),
        name="afno",
    )(x, g, area, w1, b1, w2, b2, *tables)

    def split(field):
        return field.reshape(members, cols, rows, channels).transpose(0, 2, 1, 3).astype(F32)

    weighted = (area[None, :, None, None] * cotangent.astype(F32)).astype(BF)
    output_field = (inputs.astype(F32) + split(correction)).astype(BF)
    grad_input = (weighted.astype(F32) + split(back)).astype(BF)
    return output_field, grad_input, gw1, gw2, gb1, gb2


def solution(mesh):
    return jax.shard_map(
        per_device,
        mesh=mesh,
        in_specs=(
            P("batch", "lat", "lon", None),
            P("batch", "lat", "lon", None),
            P("lat"),
            P(None, "lon", None, None),
            P(None, "lon", None),
            P(None, "lon", None, None),
            P(None, "lon", None),
        ),
        out_specs=(
            P("batch", "lat", "lon", None),
            P("batch", "lat", "lon", None),
            P(None, "lon", None, None),
            P(None, "lon", None, None),
            P(None, "lon", None),
            P(None, "lon", None),
        ),
        check_vma=False,
    )
```

```python
import functools
import math

import jax
import jax.numpy as jnp
import numpy as np
from jax import lax
from jax.experimental import pallas as pl
from jax.experimental.pallas import tpu as pltpu
from jax.sharding import PartitionSpec as P

MESH = pl.DeviceIdType.MESH
MODES = 176
LON = 360
LAT = 128
NLAT = 16
NLON = 4
ROWS = 8
COLS = LON // NLON
AREA = COLS * ROWS
KL = 11
LAG_B, LAG_C = 2, 4
CHUNKS = 8
HALF = 4
SPAN = 2 * MODES
LINES = KL * LAT
BF = jnp.bfloat16
F32 = jnp.float32


def build_tables():
    w = np.arange(LON)[:, None]
    k = np.arange(MODES)[None, :]
    angle = (w * k % LON).astype(np.float32) * np.float32(2.0 * math.pi / LON)
    cos = np.cos(angle) / math.sqrt(LON)
    sin = np.sin(angle) / math.sqrt(LON)
    weight = np.where(k == 0, 1.0, 2.0)
    forward = np.concatenate([cos, -sin], axis=1)
    back = np.concatenate([weight * cos, -weight * sin], axis=1)
    h = np.arange(LAT)
    angle = (h[:, None] * h[None, :] % LAT).astype(np.float32) * np.float32(2.0 * math.pi / LAT)
    c = np.cos(angle) / math.sqrt(LAT)
    s = np.sin(angle) / math.sqrt(LAT)
    square = np.stack([np.stack([c, -s], axis=1), np.stack([s, c], axis=1)], axis=0)
    square = square.reshape(2, NLAT, ROWS, 2, LAT).transpose(1, 0, 2, 3, 4).reshape(256, 256)
    cast = lambda a: np.asarray(a, np.float32).astype(jnp.bfloat16)
    return (
        cast(np.stack([forward.T, back.T])),
        cast(np.stack([back, forward])),
        cast(square.T),
        cast(square),
    )


def dot(a, b):
    return jnp.dot(a, b, preferred_element_type=F32)


def dot_tn(a, b):
    return lax.dot_general(a, b, (((0,), (0,)), ((), ())), preferred_element_type=F32)


def kernel(
    x_ref, g_ref, area_ref, w1_ref, b1_ref, w2_ref, b2_ref,
    lonf_hbm, lonb_hbm, latf_ref, latb_ref,
    outx_ref, outg_ref, gw_ref, gb_ref,
    lonf, lonb,
    ybuf, l1s, l1r, l2s, l2r, y2s, tmp, tmp2, cells, cells2,
    sa, hs, gps, sls, shb, dbuf1, dbuf2, wc, wt, bias, acc1, acc2, accb,
    gsend, grecv, xs, xr, ag, brows,
    y1_s, y1_r, l1_s, l1_r, l2_s, l2_r, y2_s, y2_r, t_s, g_s, g_r, p_s, p_r, a_s, a_r,
):
    me = lax.axis_index("lat")
    col = lax.axis_index("lon")
    member = lax.axis_index("batch")

    tables = [
        pltpu.make_async_copy(src, dst, t_s.at[i])
        for i, (src, dst) in enumerate(
            ((lonf_hbm, lonf), (lonb_hbm, lonb))
        )
    ]
    for copy in tables:
        copy.start()

    barrier = pltpu.get_barrier_semaphore()

    def greet_lat(i, _):
        pl.semaphore_signal(
            barrier, inc=1, device_id={"lat": lax.rem(me + i, NLAT)}, device_id_type=MESH
        )
        return 0

    lax.fori_loop(1, NLAT, greet_lat, 0)
    for i in range(1, NLON):
        pl.semaphore_signal(
            barrier, inc=1, device_id={"lon": lax.rem(col + i, NLON)}, device_id_type=MESH
        )
    pl.semaphore_signal(barrier, inc=1, device_id={"batch": 1 - member}, device_id_type=MESH)
    pl.semaphore_wait(barrier, NLAT - 1 + NLON - 1 + 1)

    def place(t):
        c = lax.rem(t, HALF)
        return c // 2, lax.rem(c, 2)

    def y1_from(t, field):
        b, n = place(t)
        for i in (2, 1, 3, 0):
            j = lax.rem(col + i, NLON)
            lanes = pl.ds(pl.multiple_of((2 * j + n) * 128, 128), 128)
            src, dst = field.at[b, :, lanes], ybuf.at[t, col]
            if i:
                pltpu.make_async_remote_copy(
                    src, dst, y1_s.at[t], y1_r.at[t],
                    device_id={"lon": j}, device_id_type=MESH,
                ).start()
            else:
                pltpu.make_async_copy(src, dst, y1_r.at[t]).start()

    def y1_send(t):
        @pl.when(t < HALF)
        def _():
            y1_from(t, x_ref)

        @pl.when(t >= HALF)
        def _():
            y1_from(t, g_ref)

    def wait_bytes(ref, sem):
        pltpu.make_async_copy(ref, ref, sem).wait()

    y1_send(0)
    y1_send(1)

    for i, ref in enumerate((w1_ref, w2_ref)):
        for n in range(2):
            re = ref[0, n].astype(F32)
            im = ref[1, n].astype(F32)
            whole = jnp.concatenate(
                [jnp.concatenate([re, im], axis=1), jnp.concatenate([-im, re], axis=1)], axis=0
            )
            wc[i, n] = whole.astype(BF)
            wt[i, n] = whole.T.astype(BF)
    for i, ref in enumerate((b1_ref, b2_ref)):
        for n in range(2):
            for q in range(2):
                bias[i, n, :, q * 128 : (q + 1) * 128] = ref[q, n : n + 1].astype(F32)
    acc1[...] = jnp.zeros_like(acc1)
    acc2[...] = jnp.zeros_like(acc2)
    accb[...] = jnp.zeros_like(accb)
    for copy in tables:
        copy.wait()

    def stage_a(t):
        kind = t // HALF
        slot = lax.rem(t, 2)
        wait_bytes(ybuf.at[t], y1_r.at[t])

        @pl.when(t + 2 < CHUNKS)
        def _():
            y1_send(t + 2)

        for j in range(NLON):
            cells[j * AREA : (j + 1) * AREA, :] = ybuf[t, j].astype(F32)

        def rows(i, _):
            h = 2 * i
            field = jnp.concatenate(
                [cells[pl.ds(h + q, LON, stride=ROWS), :].astype(BF) for q in range(2)], axis=1
            )
            modes = dot(lonf[kind], field)
            for q in range(2):
                scale = jnp.where(kind == 0, 1.0, area_ref[h + q])
                tmp[pl.ds(h + q, SPAN, stride=ROWS), :] = modes[:, q * 128 : (q + 1) * 128] * scale
            return 0

        lax.fori_loop(0, ROWS // 2, rows, 0)

        @pl.when(t >= 2)
        def _():
            wait_bytes(l1s.at[slot, pl.ds(0, NLAT - 1)], l1_s.at[t - 2])

        def peer(i, _):
            l = lax.rem(me + i, NLAT)
            at = pl.multiple_of(l * (KL * ROWS), ROWS)
            both = [
                tmp[pl.ds(at + p * (MODES * ROWS), KL * ROWS), :].reshape(KL, ROWS, 128)
                for p in range(2)
            ]
            l1s[slot, l] = jnp.concatenate(both, axis=1).astype(BF)

            @pl.when(i > 0)
            def _():
                pltpu.make_async_remote_copy(
                    l1s.at[slot, l], l1r.at[t, me], l1_s.at[t], l1_r.at[t],
                    device_id={"lat": l}, device_id_type=MESH,
                ).start()

            return 0

        lax.fori_loop(0, NLAT, peer, 0)
        l1r[t, me] = l1s[slot, me]

    def lat_forward(t, out, at):
        def one(k, _):
            z = l1r[t, :, k].reshape(256, 128)
            sp = dot(latf_ref[...], z).astype(BF)
            rows = pl.ds(pl.multiple_of(k * LAT, LAT), LAT)
            view = out.at[at] if at is not None else out
            view[rows, 0:128] = sp[:128]
            view[rows, 128:256] = sp[128:]
            return 0

        lax.fori_loop(0, KL, one, 0)

    def lat_back(t, slot):
        @pl.when(t >= 2)
        def _():
            wait_bytes(l2s.at[slot, pl.ds(0, NLAT - 1)], l2_s.at[t - 2])

        def one(k, _):
            rows = pl.ds(pl.multiple_of(k * LAT, LAT), LAT)
            s = jnp.concatenate([shb[rows, 0:128], shb[rows, 128:256]], axis=0)
            l2s[slot, :, k] = dot(latb_ref[...], s).astype(BF).reshape(NLAT, 16, 128)
            return 0

        lax.fori_loop(0, KL, one, 0)

        def peer(i, _):
            l = lax.rem(me + i, NLAT)
            pltpu.make_async_remote_copy(
                l2s.at[slot, l], l2r.at[t, me], l2_s.at[t], l2_r.at[t],
                device_id={"lat": l}, device_id_type=MESH,
            ).start()
            return 0

        lax.fori_loop(1, NLAT, peer, 0)
        l2r[t, me] = l2s[slot, me]

    BLOCK = 176
    C0 = math.sqrt(2.0 / math.pi)
    C1 = C0 * 0.044715

    def stage_b_forward(t):
        n = lax.rem(t, 2)
        slot = lax.rem(t, 2)
        lat_forward(t, sa, t)

        def one(i, _):
            rows = pl.ds(pl.multiple_of(i * BLOCK, 16), BLOCK)
            u = dot(sa[t, rows], wc[0, n]) + bias[0, n]
            sq = u * u
            th = jnp.tanh(u * (C0 + C1 * sq))
            half = 0.5 + 0.5 * th
            hid = (u * half).astype(BF)
            hs[t, rows] = hid
            gps[t, rows] = half + (0.5 * u) * (1.0 - th * th) * (C0 + (3.0 * C1) * sq)
            o = dot(hid, wc[1, n]) + bias[1, n]
            slope = jnp.tanh(o * 4.0)
            sls[t, rows] = slope * slope
            shb[rows] = (o - 0.25 * slope).astype(BF)
            return 0

        lax.fori_loop(0, LINES // BLOCK, one, 0)
        lat_back(t, slot)

    def stage_b_backward(t):
        c = t - HALF
        n = lax.rem(t, 2)
        slot = lax.rem(t, 2)
        lat_forward(t, dbuf2, None)

        def one(i, _):
            rows = pl.ds(pl.multiple_of(i * BLOCK, 16), BLOCK)
            d = (dbuf2[rows].astype(F32) * sls[c, rows]).astype(BF)
            dbuf2[rows] = d
            dp = (dot(d, wt[1, n]) * gps[c, rows]).astype(BF)
            dbuf1[rows] = dp
            shb[rows] = dot(dp, wt[0, n]).astype(BF)
            accb[n, 0] += jnp.sum(dp.astype(F32), axis=0, keepdims=True)
            accb[n, 1] += jnp.sum(d.astype(F32), axis=0, keepdims=True)
            return 0

        lax.fori_loop(0, LINES // BLOCK, one, 0)
        lat_back(t, slot)
        acc1[n] += dot_tn(sa[c], dbuf1[...])
        acc2[n] += dot_tn(hs[c], dbuf2[...])

    def stage_c(t):
        kind = t // HALF
        slot = lax.rem(t, 2)
        b, n = place(t)
        wait_bytes(l2r.at[t, pl.ds(0, NLAT - 1)], l2_r.at[t])

        def peer(l, _):
            v = l2r[t, l].astype(F32)
            at = pl.multiple_of(l * (KL * ROWS), ROWS)
            for p in range(2):
                half = v[:, p * ROWS : (p + 1) * ROWS].reshape(KL * ROWS, 128)
                tmp2[pl.ds(at + p * (MODES * ROWS), KL * ROWS), :] = half
            return 0

        lax.fori_loop(0, NLAT, peer, 0)

        @pl.when(t >= 2)
        def _():
            wait_bytes(y2s.at[slot], y2_s.at[t - 2])

        def rows(i, _):
            h = 2 * i
            modes = jnp.concatenate(
                [tmp2[pl.ds(h + q, SPAN, stride=ROWS), :].astype(BF) for q in range(2)], axis=1
            )
            field = dot(lonb[kind], modes)
            for q in range(2):
                cells2[pl.ds(h + q, LON, stride=ROWS), :] = field[:, q * 128 : (q + 1) * 128]
            return 0

        lax.fori_loop(0, ROWS // 2, rows, 0)
        for j in range(NLON):
            y2s[slot, j] = cells2[j * AREA : (j + 1) * AREA, :].astype(BF)
        lanes = pl.ds(pl.multiple_of((2 * col + n) * 128, 128), 128)

        def y2_to(out):
            for i in (2, 1, 3, 0):
                j = lax.rem(col + i, NLON)
                src, dst = y2s.at[slot, j], out.at[b, :, lanes]
                if i:
                    pltpu.make_async_remote_copy(
                        src, dst, y2_s.at[t], y2_r.at[t],
                        device_id={"lon": j}, device_id_type=MESH,
                    ).start()
                else:
                    pltpu.make_async_copy(src, dst, y2_s.at[t]).start()

        @pl.when(kind == 0)
        def _():
            y2_to(outx_ref)

        @pl.when(kind == 1)
        def _():
            y2_to(outg_ref)

    def scatter_grads():
        gsend[...] = jnp.zeros_like(gsend)
        brows[...] = jnp.zeros_like(brows)
        for which, acc in enumerate((acc1, acc2)):
            for n in range(2):
                a = acc[n]
                parts = (
                    a[:128, :128] + a[128:, 128:],
                    a[:128, 128:] - a[128:, :128],
                )
                for q in range(2):
                    at = (which * 2 + q) * 2 + n
                    part = parts[q].astype(BF)
                    gsend[2 * at, 0:64] = part[:64]
                    gsend[2 * at + 1, 0:64] = part[64:]
                    brows[at : at + 1, :] = accb[n, which, :, q * 128 : (q + 1) * 128]
        gsend[0, 64:80] = brows[...].astype(BF)

        def peer(i, _):
            l = lax.rem(me + i, NLAT)
            pltpu.make_async_remote_copy(
                gsend.at[l], grecv.at[me], g_s, g_r,
                device_id={"lat": l}, device_id_type=MESH,
            ).start()
            return 0

        lax.fori_loop(1, NLAT, peer, 0)
        grecv[me] = gsend[me]

    def finish_grads():
        wait_bytes(grecv.at[pl.ds(0, NLAT - 1)], g_r)
        part = grecv[0].astype(F32)
        for l in range(1, NLAT):
            part = part + grecv[l].astype(F32)
        xs[...] = part
        swap = pltpu.make_async_remote_copy(
            xs, xr, p_s, p_r, device_id={"batch": 1 - member}, device_id_type=MESH
        )
        swap.start()
        swap.wait()
        factor = 1.0 / math.sqrt(4 * LAT * MODES)
        ag[me] = ((xs[...] + xr[...]) * factor).astype(BF)

        def peer(i, _):
            l = lax.rem(me + i, NLAT)
            pltpu.make_async_remote_copy(
                ag.at[me], ag.at[me], a_s, a_r,
                device_id={"lat": l}, device_id_type=MESH,
            ).start()
            return 0

        lax.fori_loop(1, NLAT, peer, 0)
        wait_bytes(ag.at[pl.ds(0, NLAT - 1)], a_r)
        for l in range(NLAT):
            gw_ref[l * 64 : (l + 1) * 64, :] = ag[l, 0:64].astype(F32)
        gb_ref[...] = ag[0, 64:80].astype(F32)[:8]
        wait_bytes(ag.at[pl.ds(0, NLAT - 1)], a_s)
        wait_bytes(gsend.at[pl.ds(0, NLAT - 1)], g_s)

    def slot_of(s, _):
        @pl.when(s < CHUNKS)
        def _():
            stage_a(s)

        @pl.when(jnp.logical_and(s >= LAG_B, s < CHUNKS + LAG_B))
        def _():
            t = s - LAG_B
            wait_bytes(l1r.at[t, pl.ds(0, NLAT - 1)], l1_r.at[t])

            @pl.when(t < HALF)
            def _():
                stage_b_forward(t)

            @pl.when(t >= HALF)
            def _():
                stage_b_backward(t)

        @pl.when(s == CHUNKS + LAG_B - 1)
        def _():
            scatter_grads()

        @pl.when(s >= LAG_C)
        def _():
            stage_c(s - LAG_C)

        return 0

    lax.fori_loop(0, CHUNKS + LAG_C, slot_of, 0)
    finish_grads()
    for t in range(CHUNKS):
        wait_bytes(ybuf.at[t, pl.ds(0, NLON - 1)], y1_s.at[t])
        wait_bytes(ybuf.at[t, pl.ds(0, NLON - 1)], y2_r.at[t])
    for t in (CHUNKS - 2, CHUNKS - 1):
        wait_bytes(l1s.at[t % 2, pl.ds(0, NLAT - 1)], l1_s.at[t])
        wait_bytes(l2s.at[t % 2, pl.ds(0, NLAT - 1)], l2_s.at[t])
        wait_bytes(y2s.at[t % 2], y2_s.at[t])


def add_kernel(area_ref, x_ref, correction_ref, g_ref, back_ref, field_ref, grad_ref):
    _, rows, channels = x_ref.shape
    field_ref[0] = (x_ref[0].astype(F32) + correction_ref[0].astype(F32)).astype(BF)
    h = lax.broadcasted_iota(jnp.int32, (ROWS, channels), 0)
    scale = jnp.zeros((ROWS, channels), F32)
    for q in range(ROWS):
        scale = jnp.where(h == q, area_ref[q], scale)
    g = g_ref[0].astype(F32).reshape(rows // ROWS, ROWS, channels)
    weighted = (g * scale).astype(BF).astype(F32).reshape(rows, channels)
    grad_ref[0] = (weighted + back_ref[0].astype(F32)).astype(BF)


def per_device(inputs, cotangent, area, w1, b1, w2, b2):
    members, rows, cols, channels = inputs.shape
    tables = [jnp.asarray(a) for a in build_tables()]

    def merged(field):
        return field.transpose(0, 2, 1, 3).reshape(members, cols * rows, channels)

    x, g = merged(inputs), merged(cotangent)
    anywhere = pl.BlockSpec(memory_space=pl.ANY)
    vmem = pl.BlockSpec(memory_space=pltpu.VMEM)
    smem = pl.BlockSpec(memory_space=pltpu.SMEM)
    dma = pltpu.SemaphoreType.DMA
    V = pltpu.VMEM
    correction, back, gw, gb = pl.pallas_call(
        kernel,
        out_shape=(
            jax.ShapeDtypeStruct(x.shape, BF),
            jax.ShapeDtypeStruct(g.shape, BF),
            jax.ShapeDtypeStruct((1024, 128), F32),
            jax.ShapeDtypeStruct((8, 128), F32),
        ),
        in_specs=[anywhere] * 2 + [smem] + [vmem] * 4 + [anywhere] * 2 + [vmem] * 2,
        out_specs=(anywhere, anywhere, vmem, vmem),
        scratch_shapes=[
            V((2, SPAN, LON), BF),
            V((2, LON, SPAN), BF),
            V((CHUNKS, NLON, AREA, 128), BF),
            V((2, NLAT, KL, 16, 128), BF),
            V((CHUNKS, NLAT, KL, 16, 128), BF),
            V((2, NLAT, KL, 16, 128), BF),
            V((CHUNKS, NLAT, KL, 16, 128), BF),
            V((2, NLON, AREA, 128), BF),
            V((ROWS * SPAN, 128), F32),
            V((ROWS * SPAN, 128), F32),
            V((LON * ROWS, 128), F32),
            V((LON * ROWS, 128), F32),
            V((HALF, LINES, 256), BF),
            V((HALF, LINES, 256), BF),
            V((HALF, LINES, 256), F32),
            V((HALF, LINES, 256), F32),
            V((LINES, 256), BF),
            V((LINES, 256), BF),
            V((LINES, 256), BF),
            V((2, 2, 256, 256), BF),
            V((2, 2, 256, 256), BF),
            V((2, 2, 1, 256), F32),
            V((2, 256, 256), F32),
            V((2, 256, 256), F32),
            V((2, 2, 1, 256), F32),
            V((NLAT, 80, 128), BF),
            V((NLAT, 80, 128), BF),
            V((80, 128), F32),
            V((80, 128), F32),
            V((NLAT, 80, 128), BF),
            V((16, 128), F32),
        ]
        + [dma((CHUNKS,))] * 8
        + [dma((2,))]
        + [dma(())] * 6,
        compiler_params=pltpu.CompilerParams(
            collective_id=0, has_side_effects=True, vmem_limit_bytes=60 * 2**20
        ),
        name="afno",
    )(x, g, area, w1, b1, w2, b2, *tables)

    block = pl.BlockSpec((1, AREA // 5, channels), lambda i, j: (i, j, 0))
    output_field, grad_input = pl.pallas_call(
        add_kernel,
        grid=(members, 5),
        out_shape=(jax.ShapeDtypeStruct(x.shape, BF), jax.ShapeDtypeStruct(g.shape, BF)),
        in_specs=[smem] + [block] * 4,
        out_specs=(block, block),
        compiler_params=pltpu.CompilerParams(vmem_limit_bytes=60 * 2**20),
        name="adds",
    )(area, x, correction, g, back)

    def split(field):
        return field.reshape(members, cols, rows, channels).transpose(0, 2, 1, 3)

    gw = gw.reshape(2, 2, 2, 128, 128)
    gb = gb.reshape(2, 2, 2, 128)
    return split(output_field), split(grad_input), gw[0], gw[1], gb[0], gb[1]


def solution(mesh):
    return jax.shard_map(
        per_device,
        mesh=mesh,
        in_specs=(
            P("batch", "lat", "lon", None),
            P("batch", "lat", "lon", None),
            P("lat"),
            P(None, "lon", None, None),
            P(None, "lon", None),
            P(None, "lon", None, None),
            P(None, "lon", None),
        ),
        out_specs=(
            P("batch", "lat", "lon", None),
            P("batch", "lat", "lon", None),
            P(None, "lon", None, None),
            P(None, "lon", None, None),
            P(None, "lon", None),
            P(None, "lon", None),
        ),
        check_vma=False,
    )
```

```python
import functools
import math

import jax
import jax.numpy as jnp
import numpy as np
from jax import lax
from jax.experimental import pallas as pl
from jax.experimental.pallas import tpu as pltpu
from jax.sharding import PartitionSpec as P

MESH = pl.DeviceIdType.MESH
MODES = 176
LON = 360
LAT = 128
NLAT = 16
NLON = 4
ROWS = 8
COLS = LON // NLON
AREA = COLS * ROWS
KL = 11
LAG_B, LAG_C = 2, 4
CHUNKS = 8
HALF = 4
SPAN = 2 * MODES
LINES = KL * LAT
BF = jnp.bfloat16
F32 = jnp.float32


def build_tables():
    w = np.arange(LON)[:, None]
    k = np.arange(MODES)[None, :]
    angle = (w * k % LON).astype(np.float32) * np.float32(2.0 * math.pi / LON)
    cos = np.cos(angle) / math.sqrt(LON)
    sin = np.sin(angle) / math.sqrt(LON)
    weight = np.where(k == 0, 1.0, 2.0)
    forward = np.concatenate([cos, -sin], axis=1)
    back = np.concatenate([weight * cos, -weight * sin], axis=1)
    h = np.arange(LAT)
    angle = (h[:, None] * h[None, :] % LAT).astype(np.float32) * np.float32(2.0 * math.pi / LAT)
    c = np.cos(angle) / math.sqrt(LAT)
    s = np.sin(angle) / math.sqrt(LAT)
    square = np.stack([np.stack([c, -s], axis=1), np.stack([s, c], axis=1)], axis=0)
    square = square.reshape(2, NLAT, ROWS, 2, LAT).transpose(1, 0, 2, 3, 4).reshape(256, 256)
    cast = lambda a: np.asarray(a, np.float32).astype(jnp.bfloat16)
    return (
        cast(np.stack([forward.T, back.T])),
        cast(np.stack([back, forward])),
        cast(square.T),
        cast(square),
    )


def dot(a, b):
    return jnp.dot(a, b, preferred_element_type=F32)


def dot_tn(a, b):
    return lax.dot_general(a, b, (((0,), (0,)), ((), ())), preferred_element_type=F32)


def kernel(
    x_ref, g_ref, area_ref, w1_ref, b1_ref, w2_ref, b2_ref,
    lonf_hbm, lonb_hbm, latf_ref, latb_ref,
    outx_ref, outg_ref, gw_ref, gb_ref,
    lonf, lonb,
    ybuf, l1s, l1r, l2s, l2r, y2s, tmp, cells,
    sa, hs, gps, sls, shb, dbuf1, dbuf2, wc, wt, bias, acc1, acc2, accb,
    gsend, grecv, xs, xr, ag, brows,
    y1_s, y1_r, l1_s, l1_r, l2_s, l2_r, y2_s, y2_r, t_s, g_s, g_r, p_s, p_r, a_s, a_r,
):
    me = lax.axis_index("lat")
    col = lax.axis_index("lon")
    member = lax.axis_index("batch")

    tables = [
        pltpu.make_async_copy(src, dst, t_s.at[i])
        for i, (src, dst) in enumerate(
            ((lonf_hbm, lonf), (lonb_hbm, lonb))
        )
    ]
    for copy in tables:
        copy.start()

    barrier = pltpu.get_barrier_semaphore()

    def greet_lat(i, _):
        pl.semaphore_signal(
            barrier, inc=1, device_id={"lat": lax.rem(me + i, NLAT)}, device_id_type=MESH
        )
        return 0

    lax.fori_loop(1, NLAT, greet_lat, 0)
    for i in range(1, NLON):
        pl.semaphore_signal(
            barrier, inc=1, device_id={"lon": lax.rem(col + i, NLON)}, device_id_type=MESH
        )
    pl.semaphore_signal(barrier, inc=1, device_id={"batch": 1 - member}, device_id_type=MESH)
    pl.semaphore_wait(barrier, NLAT - 1 + NLON - 1 + 1)

    def place(t):
        c = lax.rem(t, HALF)
        return c // 2, lax.rem(c, 2)

    def y1_from(t, field):
        b, n = place(t)
        for i in (2, 1, 3, 0):
            j = lax.rem(col + i, NLON)
            lanes = pl.ds(pl.multiple_of((2 * j + n) * 128, 128), 128)
            src, dst = field.at[b, :, lanes], ybuf.at[t, col]
            if i:
                pltpu.make_async_remote_copy(
                    src, dst, y1_s.at[t], y1_r.at[t],
                    device_id={"lon": j}, device_id_type=MESH,
                ).start()
            else:
                pltpu.make_async_copy(src, dst, y1_r.at[t]).start()

    def y1_send(t):
        @pl.when(t < HALF)
        def _():
            y1_from(t, x_ref)

        @pl.when(t >= HALF)
        def _():
            y1_from(t, g_ref)

    def wait_bytes(ref, sem):
        pltpu.make_async_copy(ref, ref, sem).wait()

    y1_send(0)
    y1_send(1)

    for i, ref in enumerate((w1_ref, w2_ref)):
        for n in range(2):
            re = ref[0, n].astype(F32)
            im = ref[1, n].astype(F32)
            whole = jnp.concatenate(
                [jnp.concatenate([re, im], axis=1), jnp.concatenate([-im, re], axis=1)], axis=0
            )
            wc[i, n] = whole.astype(BF)
            wt[i, n] = whole.T.astype(BF)
    for i, ref in enumerate((b1_ref, b2_ref)):
        for n in range(2):
            for q in range(2):
                bias[i, n, :, q * 128 : (q + 1) * 128] = ref[q, n : n + 1].astype(F32)
    acc1[...] = jnp.zeros_like(acc1)
    acc2[...] = jnp.zeros_like(acc2)
    accb[...] = jnp.zeros_like(accb)
    for copy in tables:
        copy.wait()

    def stage_a(t):
        kind = t // HALF
        slot = lax.rem(t, 2)
        wait_bytes(ybuf.at[t], y1_r.at[t])

        @pl.when(t + 2 < CHUNKS)
        def _():
            y1_send(t + 2)

        for j in range(NLON):
            cells[j * AREA : (j + 1) * AREA, :] = ybuf[t, j].astype(F32)

        def rows(i, _):
            h = 2 * i
            field = jnp.concatenate(
                [cells[pl.ds(h + q, LON, stride=ROWS), :].astype(BF) for q in range(2)], axis=1
            )
            modes = dot(lonf[kind], field)
            for q in range(2):
                scale = jnp.where(kind == 0, 1.0, area_ref[h + q])
                tmp[pl.ds(h + q, SPAN, stride=ROWS), :] = modes[:, q * 128 : (q + 1) * 128] * scale
            return 0

        lax.fori_loop(0, ROWS // 2, rows, 0)

        @pl.when(t >= 2)
        def _():
            wait_bytes(l1s.at[slot, pl.ds(0, NLAT - 1)], l1_s.at[t - 2])

        def peer(i, _):
            l = lax.rem(me + i, NLAT)
            at = pl.multiple_of(l * (KL * ROWS), ROWS)
            both = [
                tmp[pl.ds(at + p * (MODES * ROWS), KL * ROWS), :].reshape(KL, ROWS, 128)
                for p in range(2)
            ]
            l1s[slot, l] = jnp.concatenate(both, axis=1).astype(BF)

            @pl.when(i > 0)
            def _():
                pltpu.make_async_remote_copy(
                    l1s.at[slot, l], l1r.at[t, me], l1_s.at[t], l1_r.at[t],
                    device_id={"lat": l}, device_id_type=MESH,
                ).start()

            return 0

        lax.fori_loop(0, NLAT, peer, 0)
        l1r[t, me] = l1s[slot, me]

    def lat_forward(t, out, at):
        def one(k, _):
            z = l1r[t, :, k].reshape(256, 128)
            sp = dot(latf_ref[...], z).astype(BF)
            rows = pl.ds(pl.multiple_of(k * LAT, LAT), LAT)
            view = out.at[at] if at is not None else out
            view[rows, 0:128] = sp[:128]
            view[rows, 128:256] = sp[128:]
            return 0

        lax.fori_loop(0, KL, one, 0)

    def lat_back(t, slot):
        @pl.when(t >= 2)
        def _():
            wait_bytes(l2s.at[slot, pl.ds(0, NLAT - 1)], l2_s.at[t - 2])

        def one(k, _):
            rows = pl.ds(pl.multiple_of(k * LAT, LAT), LAT)
            s = jnp.concatenate([shb[rows, 0:128], shb[rows, 128:256]], axis=0)
            l2s[slot, :, k] = dot(latb_ref[...], s).astype(BF).reshape(NLAT, 16, 128)
            return 0

        lax.fori_loop(0, KL, one, 0)

        def peer(i, _):
            l = lax.rem(me + i, NLAT)
            pltpu.make_async_remote_copy(
                l2s.at[slot, l], l2r.at[t, me], l2_s.at[t], l2_r.at[t],
                device_id={"lat": l}, device_id_type=MESH,
            ).start()
            return 0

        lax.fori_loop(1, NLAT, peer, 0)
        l2r[t, me] = l2s[slot, me]

    BLOCK = 176
    C0 = math.sqrt(2.0 / math.pi)
    C1 = C0 * 0.044715

    def stage_b_forward(t):
        n = lax.rem(t, 2)
        slot = lax.rem(t, 2)
        lat_forward(t, sa, t)

        def one(i, _):
            rows = pl.ds(pl.multiple_of(i * BLOCK, 16), BLOCK)
            u = dot(sa[t, rows], wc[0, n]) + bias[0, n]
            sq = u * u
            th = jnp.tanh(u * (C0 + C1 * sq))
            half = 0.5 + 0.5 * th
            hid = (u * half).astype(BF)
            hs[t, rows] = hid
            gps[t, rows] = (half + (0.5 * u) * (1.0 - th * th) * (C0 + (3.0 * C1) * sq)).astype(BF)
            o = dot(hid, wc[1, n]) + bias[1, n]
            slope = jnp.tanh(o * 4.0)
            sls[t, rows] = (slope * slope).astype(BF)
            shb[rows] = (o - 0.25 * slope).astype(BF)
            return 0

        lax.fori_loop(0, LINES // BLOCK, one, 0)
        lat_back(t, slot)

    def stage_b_backward(t):
        c = t - HALF
        n = lax.rem(t, 2)
        slot = lax.rem(t, 2)
        lat_forward(t, dbuf2, None)

        def one(i, _):
            rows = pl.ds(pl.multiple_of(i * BLOCK, 16), BLOCK)
            d = (dbuf2[rows].astype(F32) * sls[c, rows].astype(F32)).astype(BF)
            dbuf2[rows] = d
            dp = (dot(d, wt[1, n]) * gps[c, rows].astype(F32)).astype(BF)
            dbuf1[rows] = dp
            shb[rows] = dot(dp, wt[0, n]).astype(BF)
            accb[n, 0] += jnp.sum(dp.astype(F32), axis=0, keepdims=True)
            accb[n, 1] += jnp.sum(d.astype(F32), axis=0, keepdims=True)
            return 0

        lax.fori_loop(0, LINES // BLOCK, one, 0)
        lat_back(t, slot)
        acc1[n] += dot_tn(sa[c], dbuf1[...])
        acc2[n] += dot_tn(hs[c], dbuf2[...])

    def stage_c(t):
        kind = t // HALF
        slot = lax.rem(t, 2)
        b, n = place(t)
        wait_bytes(l2r.at[t, pl.ds(0, NLAT - 1)], l2_r.at[t])

        def peer(l, _):
            v = l2r[t, l].astype(F32)
            at = pl.multiple_of(l * (KL * ROWS), ROWS)
            for p in range(2):
                half = v[:, p * ROWS : (p + 1) * ROWS].reshape(KL * ROWS, 128)
                tmp[pl.ds(at + p * (MODES * ROWS), KL * ROWS), :] = half
            return 0

        lax.fori_loop(0, NLAT, peer, 0)

        @pl.when(t >= 2)
        def _():
            wait_bytes(y2s.at[slot], y2_s.at[t - 2])

        def rows(i, _):
            h = 2 * i
            modes = jnp.concatenate(
                [tmp[pl.ds(h + q, SPAN, stride=ROWS), :].astype(BF) for q in range(2)], axis=1
            )
            field = dot(lonb[kind], modes)
            for q in range(2):
                cells[pl.ds(h + q, LON, stride=ROWS), :] = field[:, q * 128 : (q + 1) * 128]
            return 0

        lax.fori_loop(0, ROWS // 2, rows, 0)
        for j in range(NLON):
            y2s[slot, j] = cells[j * AREA : (j + 1) * AREA, :].astype(BF)
        lanes = pl.ds(pl.multiple_of((2 * col + n) * 128, 128), 128)

        def y2_to(out):
            for i in (2, 1, 3, 0):
                j = lax.rem(col + i, NLON)
                src, dst = y2s.at[slot, j], out.at[b, :, lanes]
                if i:
                    pltpu.make_async_remote_copy(
                        src, dst, y2_s.at[t], y2_r.at[t],
                        device_id={"lon": j}, device_id_type=MESH,
                    ).start()
                else:
                    pltpu.make_async_copy(src, dst, y2_s.at[t]).start()

        @pl.when(kind == 0)
        def _():
            y2_to(outx_ref)

        @pl.when(kind == 1)
        def _():
            y2_to(outg_ref)

    def scatter_grads():
        gsend[...] = jnp.zeros_like(gsend)
        brows[...] = jnp.zeros_like(brows)
        for which, acc in enumerate((acc1, acc2)):
            for n in range(2):
                a = acc[n]
                parts = (
                    a[:128, :128] + a[128:, 128:],
                    a[:128, 128:] - a[128:, :128],
                )
                for q in range(2):
                    at = (which * 2 + q) * 2 + n
                    part = parts[q].astype(BF)
                    gsend[2 * at, 0:64] = part[:64]
                    gsend[2 * at + 1, 0:64] = part[64:]
                    brows[at : at + 1, :] = accb[n, which, :, q * 128 : (q + 1) * 128]
        gsend[0, 64:80] = brows[...].astype(BF)

        def peer(i, _):
            l = lax.rem(me + i, NLAT)
            pltpu.make_async_remote_copy(
                gsend.at[l], grecv.at[me], g_s, g_r,
                device_id={"lat": l}, device_id_type=MESH,
            ).start()
            return 0

        lax.fori_loop(1, NLAT, peer, 0)
        grecv[me] = gsend[me]

    def finish_grads():
        wait_bytes(grecv.at[pl.ds(0, NLAT - 1)], g_r)
        part = grecv[0].astype(F32)
        for l in range(1, NLAT):
            part = part + grecv[l].astype(F32)
        xs[...] = part
        swap = pltpu.make_async_remote_copy(
            xs, xr, p_s, p_r, device_id={"batch": 1 - member}, device_id_type=MESH
        )
        swap.start()
        swap.wait()
        factor = 1.0 / math.sqrt(4 * LAT * MODES)
        ag[me] = ((xs[...] + xr[...]) * factor).astype(BF)

        def peer(i, _):
            l = lax.rem(me + i, NLAT)
            pltpu.make_async_remote_copy(
                ag.at[me], ag.at[me], a_s, a_r,
                device_id={"lat": l}, device_id_type=MESH,
            ).start()
            return 0

        lax.fori_loop(1, NLAT, peer, 0)
        wait_bytes(ag.at[pl.ds(0, NLAT - 1)], a_r)
        for l in range(NLAT):
            gw_ref[l * 64 : (l + 1) * 64, :] = ag[l, 0:64].astype(F32)
        gb_ref[...] = ag[0, 64:80].astype(F32)[:8]
        wait_bytes(ag.at[pl.ds(0, NLAT - 1)], a_s)
        wait_bytes(gsend.at[pl.ds(0, NLAT - 1)], g_s)

    def slot_of(s, _):
        @pl.when(s < CHUNKS)
        def _():
            stage_a(s)

        @pl.when(jnp.logical_and(s >= LAG_B, s < CHUNKS + LAG_B))
        def _():
            t = s - LAG_B
            wait_bytes(l1r.at[t, pl.ds(0, NLAT - 1)], l1_r.at[t])

            @pl.when(t < HALF)
            def _():
                stage_b_forward(t)

            @pl.when(t >= HALF)
            def _():
                stage_b_backward(t)

        @pl.when(s == CHUNKS + LAG_B - 1)
        def _():
            scatter_grads()

        @pl.when(s >= LAG_C)
        def _():
            stage_c(s - LAG_C)

        return 0

    lax.fori_loop(0, CHUNKS + LAG_C, slot_of, 0)
    finish_grads()
    for t in range(CHUNKS):
        wait_bytes(ybuf.at[t, pl.ds(0, NLON - 1)], y1_s.at[t])
        wait_bytes(ybuf.at[t, pl.ds(0, NLON - 1)], y2_r.at[t])
    for t in (CHUNKS - 2, CHUNKS - 1):
        wait_bytes(l1s.at[t % 2, pl.ds(0, NLAT - 1)], l1_s.at[t])
        wait_bytes(l2s.at[t % 2, pl.ds(0, NLAT - 1)], l2_s.at[t])
        wait_bytes(y2s.at[t % 2], y2_s.at[t])


def add_kernel(area_ref, x_ref, correction_ref, g_ref, back_ref, field_ref, grad_ref):
    _, rows, channels = x_ref.shape
    field_ref[0] = (x_ref[0].astype(F32) + correction_ref[0].astype(F32)).astype(BF)
    h = lax.broadcasted_iota(jnp.int32, (ROWS, channels), 0)
    scale = jnp.zeros((ROWS, channels), F32)
    for q in range(ROWS):
        scale = jnp.where(h == q, area_ref[q], scale)
    g = g_ref[0].astype(F32).reshape(rows // ROWS, ROWS, channels)
    weighted = (g * scale).astype(BF).astype(F32).reshape(rows, channels)
    grad_ref[0] = (weighted + back_ref[0].astype(F32)).astype(BF)


def per_device(inputs, cotangent, area, w1, b1, w2, b2):
    members, rows, cols, channels = inputs.shape
    tables = [jnp.asarray(a) for a in build_tables()]

    def merged(field):
        return field.transpose(0, 2, 1, 3).reshape(members, cols * rows, channels)

    x, g = merged(inputs), merged(cotangent)
    anywhere = pl.BlockSpec(memory_space=pl.ANY)
    vmem = pl.BlockSpec(memory_space=pltpu.VMEM)
    smem = pl.BlockSpec(memory_space=pltpu.SMEM)
    dma = pltpu.SemaphoreType.DMA
    V = pltpu.VMEM
    correction, back, gw, gb = pl.pallas_call(
        kernel,
        out_shape=(
            jax.ShapeDtypeStruct(x.shape, BF),
            jax.ShapeDtypeStruct(g.shape, BF),
            jax.ShapeDtypeStruct((1024, 128), F32),
            jax.ShapeDtypeStruct((8, 128), F32),
        ),
        in_specs=[anywhere] * 2 + [smem] + [vmem] * 4 + [anywhere] * 2 + [vmem] * 2,
        out_specs=(anywhere, anywhere, vmem, vmem),
        scratch_shapes=[
            V((2, SPAN, LON), BF),
            V((2, LON, SPAN), BF),
            V((CHUNKS, NLON, AREA, 128), BF),
            V((2, NLAT, KL, 16, 128), BF),
            V((CHUNKS, NLAT, KL, 16, 128), BF),
            V((2, NLAT, KL, 16, 128), BF),
            V((CHUNKS, NLAT, KL, 16, 128), BF),
            V((2, NLON, AREA, 128), BF),
            V((ROWS * SPAN, 128), F32),
            V((LON * ROWS, 128), F32),
            V((HALF, LINES, 256), BF),
            V((HALF, LINES, 256), BF),
            V((HALF, LINES, 256), BF),
            V((HALF, LINES, 256), BF),
            V((LINES, 256), BF),
            V((LINES, 256), BF),
            V((LINES, 256), BF),
            V((2, 2, 256, 256), BF),
            V((2, 2, 256, 256), BF),
            V((2, 2, 1, 256), F32),
            V((2, 256, 256), F32),
            V((2, 256, 256), F32),
            V((2, 2, 1, 256), F32),
            V((NLAT, 80, 128), BF),
            V((NLAT, 80, 128), BF),
            V((80, 128), F32),
            V((80, 128), F32),
            V((NLAT, 80, 128), BF),
            V((16, 128), F32),
        ]
        + [dma((CHUNKS,))] * 8
        + [dma((2,))]
        + [dma(())] * 6,
        compiler_params=pltpu.CompilerParams(
            collective_id=0, has_side_effects=True, vmem_limit_bytes=44 * 2**20
        ),
        name="afno",
    )(x, g, area, w1, b1, w2, b2, *tables)

    block = pl.BlockSpec((1, AREA // 5, channels), lambda i, j: (i, j, 0))
    output_field, grad_input = pl.pallas_call(
        add_kernel,
        grid=(members, 5),
        out_shape=(jax.ShapeDtypeStruct(x.shape, BF), jax.ShapeDtypeStruct(g.shape, BF)),
        in_specs=[smem] + [block] * 4,
        out_specs=(block, block),
        compiler_params=pltpu.CompilerParams(vmem_limit_bytes=24 * 2**20),
        name="adds",
    )(area, x, correction, g, back)

    def split(field):
        return field.reshape(members, cols, rows, channels).transpose(0, 2, 1, 3)

    gw = gw.reshape(2, 2, 2, 128, 128)
    gb = gb.reshape(2, 2, 2, 128)
    return split(output_field), split(grad_input), gw[0], gw[1], gb[0], gb[1]


def solution(mesh):
    return jax.shard_map(
        per_device,
        mesh=mesh,
        in_specs=(
            P("batch", "lat", "lon", None),
            P("batch", "lat", "lon", None),
            P("lat"),
            P(None, "lon", None, None),
            P(None, "lon", None),
            P(None, "lon", None, None),
            P(None, "lon", None),
        ),
        out_specs=(
            P("batch", "lat", "lon", None),
            P("batch", "lat", "lon", None),
            P(None, "lon", None, None),
            P(None, "lon", None, None),
            P(None, "lon", None),
            P(None, "lon", None),
        ),
        check_vma=False,
    )
```

```python
import functools
import math

import jax
import jax.numpy as jnp
import numpy as np
from jax import lax
from jax.experimental import pallas as pl
from jax.experimental.pallas import tpu as pltpu
from jax.sharding import PartitionSpec as P

MESH = pl.DeviceIdType.MESH
MODES = 176
LON = 360
LAT = 128
NLAT = 16
NLON = 4
ROWS = 8
COLS = LON // NLON
AREA = COLS * ROWS
KL = 11
LAG_B, LAG_C = 2, 4
CHUNKS = 8
HALF = 4
SPAN = 2 * MODES
LINES = KL * LAT
LON_PAD = 368
BACK_AT = 2 * SPAN
LATF_AT = BACK_AT + 2 * LON_PAD
LATB_AT = LATF_AT + 256
BF = jnp.bfloat16
F32 = jnp.float32


def build_tables():
    w = np.arange(LON)[:, None]
    k = np.arange(MODES)[None, :]
    angle = (w * k % LON).astype(np.float32) * np.float32(2.0 * math.pi / LON)
    cos = np.cos(angle) / math.sqrt(LON)
    sin = np.sin(angle) / math.sqrt(LON)
    weight = np.where(k == 0, 1.0, 2.0)
    forward = np.concatenate([cos, -sin], axis=1)
    back = np.concatenate([weight * cos, -weight * sin], axis=1)
    h = np.arange(LAT)
    angle = (h[:, None] * h[None, :] % LAT).astype(np.float32) * np.float32(2.0 * math.pi / LAT)
    c = np.cos(angle) / math.sqrt(LAT)
    s = np.sin(angle) / math.sqrt(LAT)
    square = np.stack([np.stack([c, -s], axis=1), np.stack([s, c], axis=1)], axis=0)
    square = square.reshape(2, NLAT, ROWS, 2, LAT).transpose(1, 0, 2, 3, 4).reshape(256, 256)
    table = np.zeros((LATB_AT + 256, 384), np.float32)
    for kind, (there, home) in enumerate(((forward, back), (back, forward))):
        table[kind * SPAN : (kind + 1) * SPAN, :LON] = there.T
        at = BACK_AT + kind * LON_PAD
        table[at : at + LON, :SPAN] = home
    table[LATF_AT : LATF_AT + 256, :256] = square.T
    table[LATB_AT : LATB_AT + 256, :256] = square
    return table.astype(jnp.bfloat16)


def dot(a, b):
    return jnp.dot(a, b, preferred_element_type=F32)


def dot_tn(a, b):
    return lax.dot_general(a, b, (((0,), (0,)), ((), ())), preferred_element_type=F32)


def kernel(
    x_ref, g_ref, area_ref, w1_ref, b1_ref, w2_ref, b2_ref,
    tab_ref,
    outx_ref, outg_ref, gw_ref, gb_ref,
    ybuf, l1s, l1r, l2s, l2r, y2s, tmp, cells,
    sa, hs, gps, sls, shb, dbuf1, dbuf2, wc, wt, bias, acc1, acc2, accb,
    gsend, grecv, xs, xr, ag, brows,
    y1_s, y1_r, l1_s, l1_r, l2_s, l2_r, y2_s, y2_r, g_s, g_r, p_s, p_r, a_s, a_r,
):
    me = lax.axis_index("lat")
    col = lax.axis_index("lon")
    member = lax.axis_index("batch")

    barrier = pltpu.get_barrier_semaphore()

    def greet_lat(i, _):
        pl.semaphore_signal(
            barrier, inc=1, device_id={"lat": lax.rem(me + i, NLAT)}, device_id_type=MESH
        )
        return 0

    lax.fori_loop(1, NLAT, greet_lat, 0)
    for i in range(1, NLON):
        pl.semaphore_signal(
            barrier, inc=1, device_id={"lon": lax.rem(col + i, NLON)}, device_id_type=MESH
        )
    pl.semaphore_signal(barrier, inc=1, device_id={"batch": 1 - member}, device_id_type=MESH)
    pl.semaphore_wait(barrier, NLAT - 1 + NLON - 1 + 1)

    def place(t):
        c = lax.rem(t, HALF)
        return c // 2, lax.rem(c, 2)

    def y1_from(t, field):
        b, n = place(t)
        for i in (2, 1, 3, 0):
            j = lax.rem(col + i, NLON)
            lanes = pl.ds(pl.multiple_of((2 * j + n) * 128, 128), 128)
            src, dst = field.at[b, :, lanes], ybuf.at[t, col]
            if i:
                pltpu.make_async_remote_copy(
                    src, dst, y1_s.at[t], y1_r.at[t],
                    device_id={"lon": j}, device_id_type=MESH,
                ).start()
            else:
                pltpu.make_async_copy(src, dst, y1_r.at[t]).start()

    def y1_send(t):
        @pl.when(t < HALF)
        def _():
            y1_from(t, x_ref)

        @pl.when(t >= HALF)
        def _():
            y1_from(t, g_ref)

    def wait_bytes(ref, sem):
        pltpu.make_async_copy(ref, ref, sem).wait()

    y1_send(0)
    y1_send(1)

    for i, ref in enumerate((w1_ref, w2_ref)):
        for n in range(2):
            re = ref[0, n].astype(F32)
            im = ref[1, n].astype(F32)
            whole = jnp.concatenate(
                [jnp.concatenate([re, im], axis=1), jnp.concatenate([-im, re], axis=1)], axis=0
            )
            wc[i, n] = whole.astype(BF)
            wt[i, n] = whole.T.astype(BF)
    for i, ref in enumerate((b1_ref, b2_ref)):
        for n in range(2):
            for q in range(2):
                bias[i, n, :, q * 128 : (q + 1) * 128] = ref[q, n : n + 1].astype(F32)
    acc1[...] = jnp.zeros_like(acc1)
    acc2[...] = jnp.zeros_like(acc2)
    accb[...] = jnp.zeros_like(accb)

    def stage_a(t):
        kind = t // HALF
        slot = lax.rem(t, 2)
        wait_bytes(ybuf.at[t], y1_r.at[t])

        @pl.when(t + 2 < CHUNKS)
        def _():
            y1_send(t + 2)

        for j in range(NLON):
            cells[j * AREA : (j + 1) * AREA, :] = ybuf[t, j].astype(F32)

        def rows(i, _):
            h = 2 * i
            field = jnp.concatenate(
                [cells[pl.ds(h + q, LON, stride=ROWS), :].astype(BF) for q in range(2)], axis=1
            )
            at = pl.multiple_of(kind * SPAN, 16)
            modes = dot(tab_ref[pl.ds(at, SPAN), :LON], field)
            for q in range(2):
                scale = jnp.where(kind == 0, 1.0, area_ref[h + q])
                tmp[pl.ds(h + q, SPAN, stride=ROWS), :] = modes[:, q * 128 : (q + 1) * 128] * scale
            return 0

        lax.fori_loop(0, ROWS // 2, rows, 0)

        @pl.when(t >= 2)
        def _():
            wait_bytes(l1s.at[slot, pl.ds(0, NLAT - 1)], l1_s.at[t - 2])

        def peer(i, _):
            l = lax.rem(me + i, NLAT)
            at = pl.multiple_of(l * (KL * ROWS), ROWS)
            both = [
                tmp[pl.ds(at + p * (MODES * ROWS), KL * ROWS), :].reshape(KL, ROWS, 128)
                for p in range(2)
            ]
            l1s[slot, l] = jnp.concatenate(both, axis=1).astype(BF)

            @pl.when(i > 0)
            def _():
                pltpu.make_async_remote_copy(
                    l1s.at[slot, l], l1r.at[t, me], l1_s.at[t], l1_r.at[t],
                    device_id={"lat": l}, device_id_type=MESH,
                ).start()

            return 0

        lax.fori_loop(0, NLAT, peer, 0)
        l1r[t, me] = l1s[slot, me]

    def lat_forward(t, out, at):
        def one(k, _):
            z = l1r[t, :, k].reshape(256, 128)
            sp = dot(tab_ref[LATF_AT : LATF_AT + 256, :256], z).astype(BF)
            rows = pl.ds(pl.multiple_of(k * LAT, LAT), LAT)
            view = out.at[at] if at is not None else out
            view[rows, 0:128] = sp[:128]
            view[rows, 128:256] = sp[128:]
            return 0

        lax.fori_loop(0, KL, one, 0)

    def lat_back(t, slot):
        @pl.when(t >= 2)
        def _():
            wait_bytes(l2s.at[slot, pl.ds(0, NLAT - 1)], l2_s.at[t - 2])

        def one(k, _):
            rows = pl.ds(pl.multiple_of(k * LAT, LAT), LAT)
            s = jnp.concatenate([shb[rows, 0:128], shb[rows, 128:256]], axis=0)
            l2s[slot, :, k] = dot(tab_ref[LATB_AT : LATB_AT + 256, :256], s).astype(BF).reshape(NLAT, 16, 128)
            return 0

        lax.fori_loop(0, KL, one, 0)

        def peer(i, _):
            l = lax.rem(me + i, NLAT)
            pltpu.make_async_remote_copy(
                l2s.at[slot, l], l2r.at[t, me], l2_s.at[t], l2_r.at[t],
                device_id={"lat": l}, device_id_type=MESH,
            ).start()
            return 0

        lax.fori_loop(1, NLAT, peer, 0)
        l2r[t, me] = l2s[slot, me]

    BLOCK = 176
    C0 = math.sqrt(2.0 / math.pi)
    C1 = C0 * 0.044715

    def stage_b_forward(t):
        n = lax.rem(t, 2)
        slot = lax.rem(t, 2)
        lat_forward(t, sa, t)

        def one(i, _):
            rows = pl.ds(pl.multiple_of(i * BLOCK, 16), BLOCK)
            u = dot(sa[t, rows], wc[0, n]) + bias[0, n]
            sq = u * u
            th = jnp.tanh(u * (C0 + C1 * sq))
            half = 0.5 + 0.5 * th
            hid = (u * half).astype(BF)
            hs[t, rows] = hid
            gps[t, rows] = (half + (0.5 * u) * (1.0 - th * th) * (C0 + (3.0 * C1) * sq)).astype(BF)
            o = dot(hid, wc[1, n]) + bias[1, n]
            slope = jnp.tanh(o * 4.0)
            sls[t, rows] = (slope * slope).astype(BF)
            shb[rows] = (o - 0.25 * slope).astype(BF)
            return 0

        lax.fori_loop(0, LINES // BLOCK, one, 0)
        lat_back(t, slot)

    def stage_b_backward(t):
        c = t - HALF
        n = lax.rem(t, 2)
        slot = lax.rem(t, 2)
        lat_forward(t, dbuf2, None)

        def one(i, _):
            rows = pl.ds(pl.multiple_of(i * BLOCK, 16), BLOCK)
            d = (dbuf2[rows].astype(F32) * sls[c, rows].astype(F32)).astype(BF)
            dbuf2[rows] = d
            dp = (dot(d, wt[1, n]) * gps[c, rows].astype(F32)).astype(BF)
            dbuf1[rows] = dp
            shb[rows] = dot(dp, wt[0, n]).astype(BF)
            accb[n, 0] += jnp.sum(dp.astype(F32), axis=0, keepdims=True)
            accb[n, 1] += jnp.sum(d.astype(F32), axis=0, keepdims=True)
            return 0

        lax.fori_loop(0, LINES // BLOCK, one, 0)
        lat_back(t, slot)
        acc1[n] += dot_tn(sa[c], dbuf1[...])
        acc2[n] += dot_tn(hs[c], dbuf2[...])

    def stage_c(t):
        kind = t // HALF
        slot = lax.rem(t, 2)
        b, n = place(t)
        wait_bytes(l2r.at[t, pl.ds(0, NLAT - 1)], l2_r.at[t])

        def peer(l, _):
            v = l2r[t, l].astype(F32)
            at = pl.multiple_of(l * (KL * ROWS), ROWS)
            for p in range(2):
                half = v[:, p * ROWS : (p + 1) * ROWS].reshape(KL * ROWS, 128)
                tmp[pl.ds(at + p * (MODES * ROWS), KL * ROWS), :] = half
            return 0

        lax.fori_loop(0, NLAT, peer, 0)

        @pl.when(t >= 2)
        def _():
            wait_bytes(y2s.at[slot], y2_s.at[t - 2])

        def rows(i, _):
            h = 2 * i
            modes = jnp.concatenate(
                [tmp[pl.ds(h + q, SPAN, stride=ROWS), :].astype(BF) for q in range(2)], axis=1
            )
            at = pl.multiple_of(BACK_AT + kind * LON_PAD, 16)
            field = dot(tab_ref[pl.ds(at, LON_PAD), :SPAN], modes)[:LON]
            for q in range(2):
                cells[pl.ds(h + q, LON, stride=ROWS), :] = field[:, q * 128 : (q + 1) * 128]
            return 0

        lax.fori_loop(0, ROWS // 2, rows, 0)
        for j in range(NLON):
            y2s[slot, j] = cells[j * AREA : (j + 1) * AREA, :].astype(BF)
        lanes = pl.ds(pl.multiple_of((2 * col + n) * 128, 128), 128)

        def y2_to(out):
            for i in (2, 1, 3, 0):
                j = lax.rem(col + i, NLON)
                src, dst = y2s.at[slot, j], out.at[b, :, lanes]
                if i:
                    pltpu.make_async_remote_copy(
                        src, dst, y2_s.at[t], y2_r.at[t],
                        device_id={"lon": j}, device_id_type=MESH,
                    ).start()
                else:
                    pltpu.make_async_copy(src, dst, y2_s.at[t]).start()

        @pl.when(kind == 0)
        def _():
            y2_to(outx_ref)

        @pl.when(kind == 1)
        def _():
            y2_to(outg_ref)

    def scatter_grads():
        gsend[...] = jnp.zeros_like(gsend)
        brows[...] = jnp.zeros_like(brows)
        for which, acc in enumerate((acc1, acc2)):
            for n in range(2):
                a = acc[n]
                parts = (
                    a[:128, :128] + a[128:, 128:],
                    a[:128, 128:] - a[128:, :128],
                )
                for q in range(2):
                    at = (which * 2 + q) * 2 + n
                    part = parts[q].astype(BF)
                    gsend[2 * at, 0:64] = part[:64]
                    gsend[2 * at + 1, 0:64] = part[64:]
                    brows[at : at + 1, :] = accb[n, which, :, q * 128 : (q + 1) * 128]
        gsend[0, 64:80] = brows[...].astype(BF)

        def peer(i, _):
            l = lax.rem(me + i, NLAT)
            pltpu.make_async_remote_copy(
                gsend.at[l], grecv.at[me], g_s, g_r,
                device_id={"lat": l}, device_id_type=MESH,
            ).start()
            return 0

        lax.fori_loop(1, NLAT, peer, 0)
        grecv[me] = gsend[me]

    def finish_grads():
        wait_bytes(grecv.at[pl.ds(0, NLAT - 1)], g_r)
        part = grecv[0].astype(F32)
        for l in range(1, NLAT):
            part = part + grecv[l].astype(F32)
        xs[...] = part
        swap = pltpu.make_async_remote_copy(
            xs, xr, p_s, p_r, device_id={"batch": 1 - member}, device_id_type=MESH
        )
        swap.start()
        swap.wait()
        factor = 1.0 / math.sqrt(4 * LAT * MODES)
        ag[me] = ((xs[...] + xr[...]) * factor).astype(BF)

        def peer(i, _):
            l = lax.rem(me + i, NLAT)
            pltpu.make_async_remote_copy(
                ag.at[me], ag.at[me], a_s, a_r,
                device_id={"lat": l}, device_id_type=MESH,
            ).start()
            return 0

        lax.fori_loop(1, NLAT, peer, 0)
        wait_bytes(ag.at[pl.ds(0, NLAT - 1)], a_r)
        for l in range(NLAT):
            gw_ref[l * 64 : (l + 1) * 64, :] = ag[l, 0:64].astype(F32)
        gb_ref[...] = ag[0, 64:80].astype(F32)[:8]
        wait_bytes(ag.at[pl.ds(0, NLAT - 1)], a_s)
        wait_bytes(gsend.at[pl.ds(0, NLAT - 1)], g_s)

    def slot_of(s, _):
        @pl.when(s < CHUNKS)
        def _():
            stage_a(s)

        @pl.when(jnp.logical_and(s >= LAG_B, s < CHUNKS + LAG_B))
        def _():
            t = s - LAG_B
            wait_bytes(l1r.at[t, pl.ds(0, NLAT - 1)], l1_r.at[t])

            @pl.when(t < HALF)
            def _():
                stage_b_forward(t)

            @pl.when(t >= HALF)
            def _():
                stage_b_backward(t)

        @pl.when(s == CHUNKS + LAG_B - 1)
        def _():
            scatter_grads()

        @pl.when(s >= LAG_C)
        def _():
            stage_c(s - LAG_C)

        return 0

    lax.fori_loop(0, CHUNKS + LAG_C, slot_of, 0)
    finish_grads()
    for t in range(CHUNKS):
        wait_bytes(ybuf.at[t, pl.ds(0, NLON - 1)], y1_s.at[t])
        wait_bytes(ybuf.at[t, pl.ds(0, NLON - 1)], y2_r.at[t])
    for t in (CHUNKS - 2, CHUNKS - 1):
        wait_bytes(l1s.at[t % 2, pl.ds(0, NLAT - 1)], l1_s.at[t])
        wait_bytes(l2s.at[t % 2, pl.ds(0, NLAT - 1)], l2_s.at[t])
        wait_bytes(y2s.at[t % 2], y2_s.at[t])


def add_kernel(area_ref, x_ref, correction_ref, g_ref, back_ref, field_ref, grad_ref):
    _, rows, channels = x_ref.shape
    field_ref[0] = (x_ref[0].astype(F32) + correction_ref[0].astype(F32)).astype(BF)
    h = lax.broadcasted_iota(jnp.int32, (ROWS, channels), 0)
    scale = jnp.zeros((ROWS, channels), F32)
    for q in range(ROWS):
        scale = jnp.where(h == q, area_ref[q], scale)
    g = g_ref[0].astype(F32).reshape(rows // ROWS, ROWS, channels)
    weighted = (g * scale).astype(BF).astype(F32).reshape(rows, channels)
    grad_ref[0] = (weighted + back_ref[0].astype(F32)).astype(BF)


def per_device(inputs, cotangent, area, w1, b1, w2, b2):
    members, rows, cols, channels = inputs.shape
    table = jnp.asarray(build_tables())

    def merged(field):
        return field.transpose(0, 2, 1, 3).reshape(members, cols * rows, channels)

    x, g = merged(inputs), merged(cotangent)
    anywhere = pl.BlockSpec(memory_space=pl.ANY)
    vmem = pl.BlockSpec(memory_space=pltpu.VMEM)
    smem = pl.BlockSpec(memory_space=pltpu.SMEM)
    dma = pltpu.SemaphoreType.DMA
    V = pltpu.VMEM
    correction, back, gw, gb = pl.pallas_call(
        kernel,
        out_shape=(
            jax.ShapeDtypeStruct(x.shape, BF),
            jax.ShapeDtypeStruct(g.shape, BF),
            jax.ShapeDtypeStruct((1024, 128), F32),
            jax.ShapeDtypeStruct((8, 128), F32),
        ),
        in_specs=[anywhere] * 2 + [smem] + [vmem] * 5,
        out_specs=(anywhere, anywhere, vmem, vmem),
        scratch_shapes=[
            V((CHUNKS, NLON, AREA, 128), BF),
            V((2, NLAT, KL, 16, 128), BF),
            V((CHUNKS, NLAT, KL, 16, 128), BF),
            V((2, NLAT, KL, 16, 128), BF),
            V((CHUNKS, NLAT, KL, 16, 128), BF),
            V((2, NLON, AREA, 128), BF),
            V((ROWS * SPAN, 128), F32),
            V((LON * ROWS, 128), F32),
            V((HALF, LINES, 256), BF),
            V((HALF, LINES, 256), BF),
            V((HALF, LINES, 256), BF),
            V((HALF, LINES, 256), BF),
            V((LINES, 256), BF),
            V((LINES, 256), BF),
            V((LINES, 256), BF),
            V((2, 2, 256, 256), BF),
            V((2, 2, 256, 256), BF),
            V((2, 2, 1, 256), F32),
            V((2, 256, 256), F32),
            V((2, 256, 256), F32),
            V((2, 2, 1, 256), F32),
            V((NLAT, 80, 128), BF),
            V((NLAT, 80, 128), BF),
            V((80, 128), F32),
            V((80, 128), F32),
            V((NLAT, 80, 128), BF),
            V((16, 128), F32),
        ]
        + [dma((CHUNKS,))] * 8
        + [dma(())] * 6,
        compiler_params=pltpu.CompilerParams(
            collective_id=0, has_side_effects=True, vmem_limit_bytes=44 * 2**20
        ),
        name="afno",
    )(x, g, area, w1, b1, w2, b2, table)

    block = pl.BlockSpec((1, AREA // 5, channels), lambda i, j: (i, j, 0))
    output_field, grad_input = pl.pallas_call(
        add_kernel,
        grid=(members, 5),
        out_shape=(jax.ShapeDtypeStruct(x.shape, BF), jax.ShapeDtypeStruct(g.shape, BF)),
        in_specs=[smem] + [block] * 4,
        out_specs=(block, block),
        compiler_params=pltpu.CompilerParams(vmem_limit_bytes=24 * 2**20),
        name="adds",
    )(area, x, correction, g, back)

    def split(field):
        return field.reshape(members, cols, rows, channels).transpose(0, 2, 1, 3)

    gw = gw.reshape(2, 2, 2, 128, 128)
    gb = gb.reshape(2, 2, 2, 128)
    return split(output_field), split(grad_input), gw[0], gw[1], gb[0], gb[1]


def solution(mesh):
    return jax.shard_map(
        per_device,
        mesh=mesh,
        in_specs=(
            P("batch", "lat", "lon", None),
            P("batch", "lat", "lon", None),
            P("lat"),
            P(None, "lon", None, None),
            P(None, "lon", None),
            P(None, "lon", None, None),
            P(None, "lon", None),
        ),
        out_specs=(
            P("batch", "lat", "lon", None),
            P("batch", "lat", "lon", None),
            P(None, "lon", None, None),
            P(None, "lon", None, None),
            P(None, "lon", None),
            P(None, "lon", None),
        ),
        check_vma=False,
    )
```
